128 devices in a mesh: facet: 32 (over x, z, core), col: 4 (over y).
Axes of the slice: x: 4, y: 4, z: 4, core: 2. Of those that a mesh axis runs over, the one named last changes fastest.
Arguments:
- facets: bfloat16 [2, 32768, 1024], P(None, ('facet', 'col')), may hold values from -6 to 6
- observed: float32 [2, 128, 1024], P(None, 'col'), may hold values from -6 to 6
- uv_cells: int32 [2, 128, 1024], P(None, 'col'), may hold values from 0 to 511
- counts: int32 [128], P('col'), may hold values from 64 to 1024, as said below
Outputs:
- facet_residual: float32 [2, 32768, 1024], P(None, ('facet', 'col'))
The draws below stay inside these ranges and needn't reach their ends.
Inputs may be any that keep to these rules, and one draw needn't show every extreme that they name: Live slots of a subgrid are its first counts[s] slots; in every column some subgrid has all 1024 slots live.
All inputs are finite; a program needn't handle non-finite values.
Results may differ from the reference program's by a relative error of at most 0.008.
Values may be sent and summed in bfloat16 or wider, within the bound.
No kernel may reach another device: no remote copies, remote signals or barrier semaphores. Data moves between devices by JAX's collectives and lax.ppermute only.
A program may use at most 64 MiB of HBM per device.

```python
import math
import jax
import jax.numpy as jnp
from jax import lax

F = 1024
S = 512
IMAGE = 65536
VIS = 1024
SUB_W = 1
NFACET = 32
SUBCOL = 32
NSUB = 128
N_FACET = 32
N_COL = 4


def draw_counts(key, part):
    key_expo, key_drop, key_full = jax.random.split(key, 3)
    exponent = jax.random.randint(key_expo, (NSUB,), 0, 4)
    ceiling = VIS // jnp.left_shift(jnp.ones((NSUB,), jnp.int32), exponent)
    lowered = jax.random.randint(key_drop, (NSUB,), 0, VIS) % (ceiling // 2 + 1)
    column_rows = NSUB // SUBCOL
    shaped = (ceiling - lowered).reshape(column_rows, SUBCOL)
    chosen = jax.random.randint(key_full, (column_rows, 1), 0, SUBCOL)
    filled = jnp.where(jnp.arange(SUBCOL, dtype=jnp.int32)[None, :] == chosen, VIS, shaped)
    return filled.reshape(NSUB).astype(jnp.int32)


def touch_ends(values, key, least, high):
    longest = values.shape.index(max(values.shape))
    spots = []
    for shift in (0, 1):
        where = [jax.random.randint(jax.random.fold_in(key, axis), (), 0, length) for axis, length in enumerate(values.shape)]
        where[longest] = (where[longest] + shift) % values.shape[longest]
        spots.append(tuple(where))
    return values.at[spots[0]].set(least).at[spots[1]].set(high)


def shard_levels(stream_key, shape, cuts, low, high):
    def one(axis_at, blocks):
        draws = jax.random.uniform(jax.random.fold_in(jax.random.fold_in(stream_key, 6), axis_at), (blocks,), jnp.float32, low / len(cuts), high / len(cuts))
        return jnp.repeat(jnp.exp(draws), shape[axis_at] // blocks).reshape((-1,) + (1,) * (len(shape) - axis_at - 1))

    gain = one(*cuts[0])
    for cut in cuts[1:]:
        gain = gain * one(*cut)
    return gain


def scatter_about(key, dims, width, limit, pieces=(), held_as=jnp.bfloat16):
    values = jax.random.normal(key, dims, jnp.float32) * width
    if len(pieces) > 0:
        values = shard_levels(key, dims, pieces, -0.22, 0.18) * values
    return jnp.clip(values, min=-limit, max=limit).astype(held_as)


def setup_inputs(seed: int = 0) -> dict:
    key_of = jax.random.split(jax.random.key(seed), 5)
    return {
        "facets": scatter_about(key_of[0], (2, NFACET * F, F), 1.0, 6.0, ((1, 128),)),
        "observed": scatter_about(key_of[1], (2, NSUB, VIS), 1.0, 6.0, ((1, 4),), jnp.float32),
        "uv_cells": touch_ends(jax.random.randint(key_of[2], (2, NSUB, VIS), 0, S), jax.random.fold_in(key_of[2], 1), 0, S - 1).astype(jnp.int32),
        "counts": draw_counts(jax.random.fold_in(key_of[4], 71), 0),
    }


def multiply_mod(left_value, right_value):
    low_part = right_value % 256
    high_part = right_value // 256
    return (left_value * low_part + left_value * high_part % IMAGE * 256) % IMAGE

def taper_values(extent):
    position = (jnp.arange(extent, dtype=jnp.int32).astype(jnp.float32) + 0.5) / extent
    return 0.6 + 0.4 * jnp.sin(math.pi * position) ** 2

def unit_table(ticks, scale, modulus):
    angle = ticks.astype(jnp.float32) * (-2.0 * math.pi / modulus)
    return jnp.stack([jnp.cos(angle) * scale, jnp.sin(angle) * scale])

def row_table(facet_id, window, spacing, extent):
    cells = facet_id // 8 * extent + jnp.arange(extent, dtype=jnp.int32)
    freqs = IMAGE // window * jnp.arange(window, dtype=jnp.int32)
    ticks = multiply_mod(cells[None, :], freqs[:, None])
    weights = taper_values(extent)[None, :] / math.sqrt(extent)
    return unit_table(ticks, weights, IMAGE).astype(jnp.bfloat16)

def column_table(facet_id, columns, window, spacing, extent):
    cells = facet_id % 8 * extent + jnp.arange(extent, dtype=jnp.int32)
    anchor = columns * (IMAGE // 4) + (29 * columns + 3) % spacing
    freqs = (anchor[:, None] + spacing * jnp.arange(window, dtype=jnp.int32)[None, :]).reshape(-1)
    ticks = multiply_mod(cells[None, :], freqs[:, None])
    weights = taper_values(extent)[None, :] / math.sqrt(extent)
    return unit_table(ticks, weights, IMAGE).astype(jnp.bfloat16)

def phase_table(facet_id, subgrid_ids, spacing, extent):
    cells = facet_id // 8 * extent + jnp.arange(extent, dtype=jnp.int32)
    anchor = subgrid_ids * (IMAGE // 64) + (37 * subgrid_ids + 5) % (IMAGE * 8 // S)
    ticks = multiply_mod(cells[None, :], anchor[:, None])
    return unit_table(ticks, 1.0, IMAGE)

def facet_windows(row_tab, phases, strip):
    phase_real = phases[0][:, :, None]
    phase_imag = phases[1][:, :, None]
    strip_real = strip[0][None].astype(jnp.float32)
    strip_imag = strip[1][None].astype(jnp.float32)
    turned_real = (phase_real * strip_real - phase_imag * strip_imag).astype(jnp.bfloat16)
    turned_imag = (phase_real * strip_imag + phase_imag * strip_real).astype(jnp.bfloat16)

    def contract(table, turned):
        return jnp.einsum('ki,sil->skl', table.astype(jnp.float32), turned.astype(jnp.float32))
    window_real = contract(row_tab[0], turned_real) - contract(row_tab[1], turned_imag)
    window_imag = contract(row_tab[0], turned_imag) + contract(row_tab[1], turned_real)
    return jnp.stack([window_real, window_imag], axis=1).astype(jnp.bfloat16)

def facet_adjoint(row_tab, phases, returned):

    def contract(table, part):
        return jnp.einsum('ki,skl->sil', table.astype(jnp.float32), part.astype(jnp.float32))
    mixed_real = contract(row_tab[0], returned[:, 0]) + contract(row_tab[1], returned[:, 1])
    mixed_imag = contract(row_tab[0], returned[:, 1]) - contract(row_tab[1], returned[:, 0])

    def weigh(phase, mixed):
        return jnp.einsum('si,sil->il', phase, mixed, precision=lax.Precision.HIGHEST)
    real_part = weigh(phases[0], mixed_real) + weigh(phases[1], mixed_imag)
    imag_part = weigh(phases[0], mixed_imag) - weigh(phases[1], mixed_real)
    return jnp.stack([real_part, imag_part])

def regrid_block(subgrid_b, observed_part, first_cells, second_cells, is_live, extent):
    cell_axis = jnp.arange(extent, dtype=jnp.int32)
    left_tab = unit_table(first_cells[:, None] * cell_axis[None, :] % extent, 1.0, extent).astype(jnp.bfloat16)
    right_tab = unit_table(second_cells[:, None] * cell_axis[None, :] % extent, 1.0, extent)

    def product(alpha, beta):
        return jnp.dot(alpha, beta, preferred_element_type=jnp.float32)
    inner_real = product(left_tab[0], subgrid_b[0]) - product(left_tab[1], subgrid_b[1])
    inner_imag = product(left_tab[0], subgrid_b[1]) + product(left_tab[1], subgrid_b[0])
    predicted_real = lax.optimization_barrier(jnp.sum(inner_real * right_tab[0] - inner_imag * right_tab[1], axis=1)) / extent
    predicted_imag = lax.optimization_barrier(jnp.sum(inner_real * right_tab[1] + inner_imag * right_tab[0], axis=1)) / extent
    resid_real = jnp.where(is_live, observed_part[0] - predicted_real, 0.0)
    resid_imag = jnp.where(is_live, observed_part[1] - predicted_imag, 0.0)
    weighted_real = (resid_real[:, None] * right_tab[0] + resid_imag[:, None] * right_tab[1]).astype(jnp.bfloat16)
    weighted_imag = (resid_imag[:, None] * right_tab[0] - resid_real[:, None] * right_tab[1]).astype(jnp.bfloat16)
    regrid_real = product(left_tab[0].T, weighted_real) + product(left_tab[1].T, weighted_imag)
    regrid_imag = product(left_tab[0].T, weighted_imag) - product(left_tab[1].T, weighted_real)
    return (regrid_real, regrid_imag)

def reference(facets, observed, uv_cells, counts):
    facet_count = N_FACET
    column_count = N_COL
    per_column = SUB_W * N_FACET
    window = S // 8
    spacing = IMAGE // F
    stacked = facets.reshape(2, facet_count, F, F).transpose(1, 0, 2, 3)
    subgrid_ids = jnp.arange(per_column, dtype=jnp.int32)
    facet_ids = jnp.arange(facet_count, dtype=jnp.int32)
    accumulated = jnp.zeros((facet_count, 2, F, F), jnp.float32)
    for column_index in range(column_count):
        columns = jnp.array([column_index], jnp.int32)

        def forward(carried, item):
            facet_id, pixels = item
            colt = column_table(facet_id, columns, window, spacing, F)
            strip_real = jnp.dot(pixels[0], colt[0].T, preferred_element_type=jnp.float32) - jnp.dot(pixels[1], colt[1].T, preferred_element_type=jnp.float32)
            strip_imag = jnp.dot(pixels[0], colt[1].T, preferred_element_type=jnp.float32) + jnp.dot(pixels[1], colt[0].T, preferred_element_type=jnp.float32)
            strip = jnp.stack([strip_real, strip_imag]).astype(jnp.bfloat16)
            windows = facet_windows(row_table(facet_id, window, spacing, F), phase_table(facet_id, subgrid_ids, spacing, F), strip)
            zero_index = jnp.zeros((), jnp.int32)
            corner = (zero_index, zero_index, (facet_id % 32 // 8 * window).astype(jnp.int32), (facet_id % 8 * window).astype(jnp.int32))
            current = lax.dynamic_slice(carried, corner, (per_column, 2, window, window))
            carried = lax.dynamic_update_slice(carried, current + windows.astype(jnp.float32), corner)
            return (carried, None)
        initial = jnp.zeros((per_column, 2, S, S), jnp.float32)
        summed, unused = lax.scan(forward, initial, (facet_ids, stacked))
        subgrid_b = summed.astype(jnp.bfloat16)
        first_row = column_index * per_column
        column_obs = observed[:, first_row:first_row + per_column].transpose(1, 0, 2)
        column_uv = uv_cells[:, first_row:first_row + per_column]
        column_counts = counts[first_row:first_row + per_column]

        def per_subgrid(item):
            grid_part, observed_part, first_cells, second_cells, live_count = item
            is_live = jnp.arange(VIS, dtype=jnp.int32) < live_count
            regrid_real, regrid_imag = regrid_block(grid_part, observed_part, first_cells, second_cells, is_live, S)
            return jnp.stack([regrid_real, regrid_imag]) * (1.0 / math.sqrt(VIS))
        regridded = lax.map(per_subgrid, (subgrid_b, column_obs, column_uv[0], column_uv[1], column_counts))

        def backward(facet_id):
            colt = column_table(facet_id, columns, window, spacing, F)
            zero_index = jnp.zeros((), jnp.int32)
            corner = (zero_index, zero_index, (facet_id % 32 // 8 * window).astype(jnp.int32), (facet_id % 8 * window).astype(jnp.int32))
            returned = lax.dynamic_slice(regridded, corner, (per_column, 2, window, window)).astype(jnp.bfloat16)
            backstrip = facet_adjoint(row_table(facet_id, window, spacing, F), phase_table(facet_id, subgrid_ids, spacing, F), returned).astype(jnp.bfloat16)
            image_real = jnp.dot(backstrip[0], colt[0], preferred_element_type=jnp.float32) + jnp.dot(backstrip[1], colt[1], preferred_element_type=jnp.float32)
            image_imag = jnp.dot(backstrip[1], colt[0], preferred_element_type=jnp.float32) - jnp.dot(backstrip[0], colt[1], preferred_element_type=jnp.float32)
            return jnp.stack([image_real, image_imag])
        accumulated = accumulated + lax.map(backward, facet_ids)
    return accumulated.transpose(1, 0, 2, 3).reshape(2, facet_count * F, F)
```

```python
import math

import jax
import jax.numpy as jnp
import ml_dtypes
import numpy as np
from jax import lax
from jax.experimental import pallas as pl
from jax.experimental.pallas import tpu as pltpu
from jax.sharding import Mesh
from jax.sharding import PartitionSpec as P

F = 1024
S = 512
IMAGE = 65536
VIS = 1024
W = 64
SUBCOL = 32
N_COL = 4
FACET = ("facet_0", "facet_1", "facet_2")
FACET_COL = ("facet_0", "facet_1", "facet_2", "col")
BF = jnp.bfloat16
F32 = jnp.float32


def unit(ticks, modulus):
    angle = (ticks % modulus).astype(np.float64) * (-2.0 * math.pi / modulus)
    return np.cos(angle), np.sin(angle)


def taper():
    return 0.6 + 0.4 * np.sin(math.pi * (np.arange(F) + 0.5) / F) ** 2


def bf(values):
    return np.asarray(values, np.float32).astype(ml_dtypes.bfloat16)


def hi_lo(values):
    high = bf(values)
    return high, bf(values - high.astype(np.float64))


def column_rows():
    c, l, q = np.arange(N_COL), np.arange(W), np.arange(F)
    vc = c * (IMAGE // 4) + (29 * c + 3) % 64
    ticks = q[None, None, :] * (vc[:, None, None] + 64 * l[None, :, None])
    real, imag = unit(ticks, IMAGE)
    weights = taper() / math.sqrt(F)
    return bf(np.stack([real * weights, imag * weights], axis=1).reshape(N_COL * 2 * W, F))


def window_rows():
    j, k, p = np.arange(SUBCOL), np.arange(W), np.arange(F)
    freqs = 1024 * (k[None, :] + j[:, None]) + ((37 * j + 5) % 1024)[:, None]
    real, imag = unit(p[None, :] * freqs.reshape(-1, 1), IMAGE)
    weights = taper() / math.sqrt(F)
    return bf(np.stack([real * weights, imag * weights]))


def left_rows():
    real, imag = unit(np.arange(256)[:, None] * np.arange(S)[None, :], S)
    return bf(np.concatenate([real, imag]))


def right_rows():
    base = hi_lo(np.concatenate(unit(np.arange(W)[:, None] * np.arange(S)[None, :], S)))
    eighth = hi_lo(np.concatenate(unit(W * np.arange(8)[:, None] * np.arange(S)[None, :], S)))
    return np.concatenate([base[0], base[1], eighth[0], eighth[1]])


def facet_tables():
    return np.stack(unit(np.arange(W), W)).astype(np.float32)


def dot(a, b):
    return jnp.dot(a, b, preferred_element_type=F32)


def half_sign(shape):
    lane = lax.broadcasted_iota(jnp.int32, shape, len(shape) - 1)
    return jnp.where(lane % 128 < W, -1.0, 1.0).astype(F32)


def swap(values):
    return pltpu.roll(values, W, 1)


def scalar_phase(units, facet_row, facet_col, subgrid, column):
    shift = (37 * subgrid + 5) & 1023
    anchor = (29 * column + 3) & 63
    tick = (facet_row * shift + facet_col * anchor) & 63
    return units[0, tick], units[1, tick]


def strip_kernel(pixels, table, out):
    real = dot(pixels[0], table[...])
    imag = dot(pixels[1], table[...])
    sign = half_sign((256, 128))
    for c in range(N_COL):
        at = slice(c * 128, (c + 1) * 128)
        out[c] = (real[:, at] + sign * swap(imag[:, at])).astype(BF)


def window_kernel(units, table, strip, out):
    facet = lax.axis_index(FACET)
    column = lax.axis_index("col")
    step = pl.program_id(0)
    group = out.shape[0]
    rows = group * W
    both = dot(table[...].reshape(2 * rows, F), strip[...].reshape(F, 128))
    sign = half_sign((W, 128))
    for g in range(group):
        at = slice(g * W, (g + 1) * W)
        block = both[:rows][at] + sign * swap(both[rows:][at])
        real, imag = scalar_phase(units, facet // 8, facet % 8, step * group + g, column)
        out[g] = (block * real + sign * swap(block) * imag).astype(BF)


def subgrid_kernel(units, counts, windows, observed, cells, left_tab, right_tab, out, left, weighted):
    subgrid = lax.axis_index(FACET)
    column = lax.axis_index("col")
    count = counts[subgrid]
    turned = []
    for y in range(8):
        block = jnp.concatenate([windows[x * 8 + y] for x in range(4)], axis=0)
        block = block.astype(F32).T
        other = jnp.concatenate([-block[W:], block[:W]], axis=0)
        turned.append(jnp.concatenate([block, other], axis=1).astype(BF))
    chunk = 256
    for begin in range(0, VIS, chunk):
        at = slice(begin, begin + chunk)
        first = cells[0, pl.ds(subgrid, 1), at]
        second = cells[1, pl.ds(subgrid, 1), at]
        cell = lax.broadcasted_iota(jnp.int32, (S, chunk), 0)
        left_part = dot(left_tab[...], jnp.where(cell == first, 1.0, 0.0).astype(BF)).astype(BF)
        left[:, at] = left_part
        right = dot(right_tab[...], jnp.where(cell == second, 1.0, 0.0).astype(BF))
        base_real = right[0:64] + right[128:192]
        base_imag = right[64:128] + right[192:256]
        eighth_real = right[256:264] + right[272:280]
        eighth_imag = right[264:272] + right[280:288]
        pred_real = jnp.zeros((1, chunk), F32)
        pred_imag = jnp.zeros((1, chunk), F32)
        for y in range(8):
            inner = dot(turned[y], left_part)
            inner_real, inner_imag = inner[:W], inner[W:]
            part_real = jnp.sum(inner_real * base_real - inner_imag * base_imag, axis=0, keepdims=True)
            part_imag = jnp.sum(inner_real * base_imag + inner_imag * base_real, axis=0, keepdims=True)
            er, ei = eighth_real[y : y + 1], eighth_imag[y : y + 1]
            pred_real += part_real * er - part_imag * ei
            pred_imag += part_real * ei + part_imag * er
        slot = begin + lax.broadcasted_iota(jnp.int32, (1, chunk), 1)
        live = slot < count
        resid_real = jnp.where(live, observed[0, pl.ds(subgrid, 1), at] - pred_real / S, 0.0)
        resid_imag = jnp.where(live, observed[1, pl.ds(subgrid, 1), at] - pred_imag / S, 0.0)
        for y in range(8):
            er, ei = eighth_real[y : y + 1], eighth_imag[y : y + 1]
            turned_real = resid_real * er + resid_imag * ei
            turned_imag = resid_imag * er - resid_real * ei
            weighted[y * 128 : y * 128 + W, at] = (
                turned_real * base_real + turned_imag * base_imag
            ).astype(BF)
            weighted[y * 128 + W : (y + 1) * 128, at] = (
                turned_imag * base_real - turned_real * base_imag
            ).astype(BF)
    sign = half_sign((W, 128))
    for y in range(8):
        both = lax.dot_general(
            left[...],
            weighted[y * 128 : (y + 1) * 128],
            (((1,), (1,)), ((), ())),
            preferred_element_type=F32,
        )
        for x in range(4):
            block = both[x * W : (x + 1) * W] - sign * swap(both[256 + x * W : 256 + (x + 1) * W])
            real, imag = scalar_phase(units, x, y, subgrid, column)
            scale = 1.0 / math.sqrt(VIS)
            out[x * 8 + y] = (
                block * (real * scale) - sign * swap(block) * (imag * scale)
            ).astype(BF)


def back_kernel(table, returned, out, turned):
    @pl.when(pl.program_id(0) == 0)
    def _():
        for g in range(8):
            block = returned[g * 4 : (g + 1) * 4].reshape(256, 128)
            turned[:, g * 256 : (g + 1) * 256] = block.astype(F32).T.astype(BF)

    real = dot(turned[...], table[0])
    imag = dot(turned[...], table[1])
    out[0, :W] = (real[:W] + imag[W:]).astype(BF)
    out[0, W:] = (real[W:] - imag[:W]).astype(BF)


def image_kernel(strips, table, out):
    rows, others = [], []
    for c in range(N_COL):
        block = strips[c].astype(F32)
        other = jnp.concatenate([block[W:], -block[:W]], axis=0)
        rows.append(block.T.astype(BF))
        others.append(other.T.astype(BF))
    out[0] = dot(jnp.concatenate(rows, axis=1), table[...])
    out[1] = dot(jnp.concatenate(others, axis=1), table[...])


VMEM = pl.BlockSpec(memory_space=pltpu.VMEM)
SMEM = pl.BlockSpec(memory_space=pltpu.SMEM)


def params():
    return pltpu.CompilerParams(vmem_limit_bytes=48 * 1024 * 1024)


def on_device(facets, observed, uv_cells, counts):
    units = jnp.asarray(facet_tables())
    by_column = column_rows()
    row_tab = jnp.asarray(window_rows())
    strips = pl.pallas_call(
        strip_kernel,
        out_shape=jax.ShapeDtypeStruct((N_COL, 256, 128), BF),
        in_specs=[VMEM, VMEM],
        out_specs=VMEM,
        compiler_params=params(),
        name="strip",
    )(facets, jnp.asarray(np.ascontiguousarray(by_column.T)))
    strip = lax.all_to_all(strips, "col", split_axis=0, concat_axis=0, tiled=True)
    windows = pl.pallas_call(
        window_kernel,
        grid=(8,),
        out_shape=jax.ShapeDtypeStruct((SUBCOL, W, 128), BF),
        in_specs=[SMEM, pl.BlockSpec((2, 256, F), lambda i: (0, i, 0)), VMEM],
        out_specs=pl.BlockSpec((4, W, 128), lambda i: (i, 0, 0)),
        compiler_params=params(),
        name="window",
    )(units, row_tab, strip)
    windows = lax.all_to_all(windows, FACET, split_axis=0, concat_axis=0, tiled=True)
    returned = pl.pallas_call(
        subgrid_kernel,
        out_shape=jax.ShapeDtypeStruct((SUBCOL, W, 128), BF),
        in_specs=[SMEM, SMEM, VMEM, VMEM, VMEM, VMEM, VMEM],
        out_specs=VMEM,
        scratch_shapes=[pltpu.VMEM((S, VIS), BF), pltpu.VMEM((1024, VIS), BF)],
        compiler_params=params(),
        name="subgrid",
    )(units, counts, windows, observed, uv_cells, jnp.asarray(left_rows()), jnp.asarray(right_rows()))
    returned = lax.all_to_all(returned, FACET, split_axis=0, concat_axis=0, tiled=True)
    back = pl.pallas_call(
        back_kernel,
        grid=(4,),
        out_shape=jax.ShapeDtypeStruct((N_COL, 128, 256), BF),
        in_specs=[pl.BlockSpec((2, SUBCOL * W, 256), lambda i: (0, 0, i)), VMEM],
        out_specs=pl.BlockSpec((1, 128, 256), lambda i: (i, 0, 0)),
        scratch_shapes=[pltpu.VMEM((128, SUBCOL * W), BF)],
        compiler_params=params(),
        name="back",
    )(row_tab, returned)
    back = lax.all_to_all(back, "col", split_axis=0, concat_axis=0, tiled=True)
    return pl.pallas_call(
        image_kernel,
        out_shape=jax.ShapeDtypeStruct((2, 256, F), F32),
        in_specs=[VMEM, VMEM],
        out_specs=VMEM,
        compiler_params=params(),
        name="image",
    )(back, jnp.asarray(by_column))


def solution(mesh):
    finer = Mesh(
        mesh.devices.reshape(4, 4, 2, mesh.shape["col"]), ("facet_0", "facet_1", "facet_2", "col")
    )
    return jax.shard_map(
        on_device,
        mesh=finer,
        in_specs=(P(None, FACET_COL, None), P(None, "col", None), P(None, "col", None), P("col")),
        out_specs=P(None, FACET_COL, None),
        check_vma=False,
    )
```

```python
import math

import jax
import jax.numpy as jnp
import ml_dtypes
import numpy as np
from jax import lax
from jax.experimental import pallas as pl
from jax.experimental.pallas import tpu as pltpu
from jax.sharding import Mesh
from jax.sharding import PartitionSpec as P

F = 1024
S = 512
IMAGE = 65536
VIS = 1024
W = 64
SUBCOL = 32
N_COL = 4
FACET = ("facet_0", "facet_1", "facet_2")
FACET_COL = ("facet_0", "facet_1", "facet_2", "col")
BF = jnp.bfloat16
F32 = jnp.float32
PIECES = 4
CHUNK = 256
COST = pl.CostEstimate(flops=2 * 10**10, bytes_accessed=2**24, transcendentals=0)


def unit(ticks, modulus):
    angle = (ticks % modulus).astype(np.float64) * (-2.0 * math.pi / modulus)
    return np.cos(angle), np.sin(angle)


def taper():
    return 0.6 + 0.4 * np.sin(math.pi * (np.arange(F) + 0.5) / F) ** 2


def bf(values):
    return np.asarray(values, np.float32).astype(ml_dtypes.bfloat16)


def hi_lo(values):
    high = bf(values)
    return high, bf(values - high.astype(np.float64))


def column_rows():
    c, l, q = np.arange(N_COL), np.arange(W), np.arange(F)
    vc = c * (IMAGE // 4) + (29 * c + 3) % 64
    ticks = q[None, None, :] * (vc[:, None, None] + 64 * l[None, :, None])
    real, imag = unit(ticks, IMAGE)
    weights = taper() / math.sqrt(F)
    return bf(np.stack([real * weights, imag * weights], axis=1).reshape(N_COL * 2 * W, F))


def window_rows():
    j, k, p = np.arange(SUBCOL), np.arange(W), np.arange(F)
    freqs = 1024 * (k[None, :] + j[:, None]) + ((37 * j + 5) % 1024)[:, None]
    real, imag = unit(p[None, :] * freqs.reshape(-1, 1), IMAGE)
    weights = taper() / math.sqrt(F)
    return bf(np.stack([real * weights, imag * weights]))


def left_rows():
    real, imag = unit(np.arange(256)[:, None] * np.arange(S)[None, :], S)
    return bf(np.concatenate([real, imag]))


def right_rows():
    base = hi_lo(np.concatenate(unit(np.arange(W)[:, None] * np.arange(S)[None, :], S)))
    eighth = hi_lo(np.concatenate(unit(W * np.arange(8)[:, None] * np.arange(S)[None, :], S)))
    return np.concatenate([base[0], base[1], eighth[0], eighth[1]])


def facet_tables():
    return np.stack(unit(np.arange(W), W)).astype(np.float32)


def dot(a, b):
    return jnp.dot(a, b, preferred_element_type=F32)


def half_sign(shape):
    lane = lax.broadcasted_iota(jnp.int32, shape, len(shape) - 1)
    return jnp.where(lane % 128 < W, -1.0, 1.0).astype(F32)


def swap(values):
    return pltpu.roll(values, W, 1)


def scalar_phase(units, facet_row, facet_col, subgrid, column):
    shift = (37 * subgrid + 5) & 1023
    anchor = (29 * column + 3) & 63
    tick = (facet_row * shift + facet_col * anchor) & 63
    return units[0, tick], units[1, tick]


def column_of(shift):
    return (lax.axis_index("col") + shift) & (N_COL - 1)


def lanes(block, width):
    return pl.ds(pl.multiple_of(block * width, width), width)


def strip_kernel(pixels, table, *refs):
    outs = refs[:N_COL]
    pixels_in, table_in, held, arrived = refs[N_COL:]
    depth = F // PIECES
    copies = []
    for i in range(PIECES):
        at = slice(i * depth, (i + 1) * depth)
        copies.append(
            (
                pltpu.make_async_copy(table.at[at], table_in.at[at], arrived.at[i]),
                pltpu.make_async_copy(
                    pixels.at[:, :, at], pixels_in.at[:, :, at], arrived.at[PIECES + i]
                ),
            )
        )
    for pair in copies[:2]:
        pair[0].start()
        pair[1].start()
    both = jnp.zeros((512, 512), F32)
    for i in range(PIECES):
        copies[i][0].wait()
        copies[i][1].wait()
        if i + 2 < PIECES:
            copies[i + 2][0].start()
            copies[i + 2][1].start()
        at = slice(i * depth, (i + 1) * depth)
        both += dot(pixels_in[:, :, at].reshape(512, depth), table_in[at])
    held[...] = both
    sign = half_sign((256, 128))
    for shift, out in enumerate(outs):
        at = lanes(column_of(shift), 128)
        out[...] = (held[:256, at] + sign * swap(held[256:, at])).astype(BF)


def window_kernel(units, table, *refs):
    strips = refs[:N_COL]
    out, turned = refs[N_COL:]
    facet = lax.axis_index(FACET)
    column = lax.axis_index("col")
    for shift, strip in enumerate(strips):
        turned[:, lanes(column_of(-shift), 256)] = strip[...].astype(F32).T.astype(BF)
    sign = half_sign((W, 128))
    group = 4
    for step in range(SUBCOL // group):
        at = slice(step * group * W, (step + 1) * group * W)
        first, second = dot(turned[...], table[0, :, at]), dot(turned[...], table[1, :, at])
        both = jnp.concatenate([first[:W] - second[W:], first[W:] + second[:W]], axis=0).T
        for g in range(group):
            block = both[g * W : (g + 1) * W]
            real, imag = scalar_phase(units, facet // 8, facet % 8, step * group + g, column)
            out[step * group + g] = (block * real + sign * swap(block) * imag).astype(BF)


def wave_kernel(cells, left_tab, right_tab, left, base, eighth):
    subgrid = lax.axis_index(FACET)
    for begin in range(0, VIS, CHUNK):
        at = slice(begin, begin + CHUNK)
        first = cells[0, pl.ds(subgrid, 1), at]
        second = cells[1, pl.ds(subgrid, 1), at]
        cell = lax.broadcasted_iota(jnp.int32, (S, CHUNK), 0)
        left[:, at] = dot(left_tab[...], jnp.where(cell == first, 1.0, 0.0).astype(BF)).astype(BF)
        right = dot(right_tab[...], jnp.where(cell == second, 1.0, 0.0).astype(BF))
        base[:, at] = right[0:128] + right[128:256]
        eighth[:, at] = right[256:272] + right[272:288]


def subgrid_kernel(units, counts, windows, observed, left, base, eighth, out, weighted):
    subgrid = lax.axis_index(FACET)
    column = lax.axis_index("col")
    count = counts[subgrid]
    turned = []
    for y in range(8):
        block = jnp.concatenate([windows[x * 8 + y] for x in range(4)], axis=0)
        block = block.astype(F32).T
        other = jnp.concatenate([-block[W:], block[:W]], axis=0)
        turned.append(jnp.concatenate([block, other], axis=1).astype(BF))
    for begin in range(0, VIS, CHUNK):
        at = slice(begin, begin + CHUNK)
        left_part = left[:, at]
        base_real, base_imag = base[:W, at], base[W:, at]
        pred_real = jnp.zeros((1, CHUNK), F32)
        pred_imag = jnp.zeros((1, CHUNK), F32)
        for y in range(8):
            inner = dot(turned[y], left_part)
            inner_real, inner_imag = inner[:W], inner[W:]
            part_real = jnp.sum(inner_real * base_real - inner_imag * base_imag, axis=0, keepdims=True)
            part_imag = jnp.sum(inner_real * base_imag + inner_imag * base_real, axis=0, keepdims=True)
            er, ei = eighth[y : y + 1, at], eighth[8 + y : 9 + y, at]
            pred_real += part_real * er - part_imag * ei
            pred_imag += part_real * ei + part_imag * er
        slot = begin + lax.broadcasted_iota(jnp.int32, (1, CHUNK), 1)
        live = slot < count
        resid_real = jnp.where(live, observed[0, pl.ds(subgrid, 1), at] - pred_real / S, 0.0)
        resid_imag = jnp.where(live, observed[1, pl.ds(subgrid, 1), at] - pred_imag / S, 0.0)
        for y in range(8):
            er, ei = eighth[y : y + 1, at], eighth[8 + y : 9 + y, at]
            turned_real = resid_real * er + resid_imag * ei
            turned_imag = resid_imag * er - resid_real * ei
            weighted[y * 128 : y * 128 + W, at] = (
                turned_real * base_real + turned_imag * base_imag
            ).astype(BF)
            weighted[y * 128 + W : (y + 1) * 128, at] = (
                turned_imag * base_real - turned_real * base_imag
            ).astype(BF)
    sign = half_sign((W, 128))
    for y in range(8):
        both = lax.dot_general(
            left[...],
            weighted[y * 128 : (y + 1) * 128],
            (((1,), (1,)), ((), ())),
            preferred_element_type=F32,
        )
        for x in range(4):
            block = both[x * W : (x + 1) * W] - sign * swap(both[256 + x * W : 256 + (x + 1) * W])
            real, imag = scalar_phase(units, x, y, subgrid, column)
            scale = 1.0 / math.sqrt(VIS)
            out[x * 8 + y] = (
                block * (real * scale) - sign * swap(block) * (imag * scale)
            ).astype(BF)


def back_kernel(table, returned, *outs):
    turned = []
    for g in range(8):
        block = returned[g * 4 : (g + 1) * 4].reshape(256, 128)
        turned.append(block.astype(F32).T.astype(BF))
    turned = jnp.concatenate(turned, axis=1)
    for shift, out in enumerate(outs):
        at = lanes(column_of(shift), 256)
        real, imag = dot(turned, table[0, :, at]), dot(turned, table[1, :, at])
        out[:W] = (real[:W] + imag[W:]).astype(BF)
        out[W:] = (real[W:] - imag[:W]).astype(BF)


def image_kernel(table, *refs):
    strips = refs[:N_COL]
    out, held, wide, left = refs[N_COL:]
    for shift, strip in enumerate(strips):
        at = lanes(column_of(-shift), 128)
        block = strip[...].astype(F32)
        other = jnp.concatenate([block[W:], -block[:W]], axis=0)
        wide[:256, at] = block.T.astype(BF)
        wide[256:, at] = other.T.astype(BF)
    copies = []
    for i in range(PIECES):
        at = slice(i * 256, (i + 1) * 256)
        held[:, :, at] = dot(wide[...], table[:, at]).reshape(2, 256, 256)
        copy = pltpu.make_async_copy(held.at[:, :, at], out.at[:, :, at], left.at[i])
        copy.start()
        copies.append(copy)
    for copy in copies:
        copy.wait()


VMEM = pl.BlockSpec(memory_space=pltpu.VMEM)
SMEM = pl.BlockSpec(memory_space=pltpu.SMEM)
HBM = pl.BlockSpec(memory_space=pltpu.HBM)


def params(mebibytes=24):
    return pltpu.CompilerParams(vmem_limit_bytes=mebibytes * 1024 * 1024)


def along_columns(parts):
    arrived = list(parts)
    for shift in (2, 1, 3):
        route = [(i, (i + shift) % N_COL) for i in range(N_COL)]
        arrived[shift] = lax.ppermute(parts[shift], "col", route)
    return arrived


def shaped(*dims, dtype=BF):
    return jax.ShapeDtypeStruct(dims, dtype)


def on_device(facets, observed, uv_cells, counts):
    units = jnp.asarray(facet_tables())
    by_column = column_rows()
    by_window = window_rows()
    strips = pl.pallas_call(
        strip_kernel,
        out_shape=[shaped(256, 128)] * N_COL,
        in_specs=[HBM, HBM],
        out_specs=[VMEM] * N_COL,
        scratch_shapes=[
            pltpu.VMEM((2, 256, F), BF),
            pltpu.VMEM((F, 512), BF),
            pltpu.VMEM((512, 512), F32),
            pltpu.SemaphoreType.DMA((2 * PIECES,)),
        ],
        compiler_params=params(),
        cost_estimate=COST,
        name="strip",
    )(facets, jnp.asarray(np.ascontiguousarray(by_column.T)))
    left, base, eighth = pl.pallas_call(
        wave_kernel,
        out_shape=[shaped(S, VIS), shaped(128, VIS, dtype=F32), shaped(16, VIS, dtype=F32)],
        in_specs=[VMEM] * 3,
        out_specs=[VMEM] * 3,
        compiler_params=params(),
        cost_estimate=COST,
        name="wave",
    )(uv_cells, jnp.asarray(left_rows()), jnp.asarray(right_rows()))
    windows = pl.pallas_call(
        window_kernel,
        out_shape=shaped(SUBCOL, W, 128),
        in_specs=[SMEM, VMEM] + [VMEM] * N_COL,
        out_specs=VMEM,
        scratch_shapes=[pltpu.VMEM((128, F), BF)],
        compiler_params=params(),
        cost_estimate=COST,
        name="window",
    )(units, jnp.asarray(np.ascontiguousarray(by_window.transpose(0, 2, 1))), *along_columns(strips))
    windows = lax.all_to_all(windows, FACET, split_axis=0, concat_axis=0, tiled=True)
    returned = pl.pallas_call(
        subgrid_kernel,
        out_shape=shaped(SUBCOL, W, 128),
        in_specs=[SMEM, SMEM] + [VMEM] * 5,
        out_specs=VMEM,
        scratch_shapes=[pltpu.VMEM((1024, VIS), BF)],
        compiler_params=params(),
        cost_estimate=COST,
        name="subgrid",
    )(units, counts, windows, observed, left, base, eighth)
    returned = lax.all_to_all(returned, FACET, split_axis=0, concat_axis=0, tiled=True)
    back = pl.pallas_call(
        back_kernel,
        out_shape=[shaped(128, 256)] * N_COL,
        in_specs=[VMEM, VMEM],
        out_specs=[VMEM] * N_COL,
        compiler_params=params(),
        cost_estimate=COST,
        name="back",
    )(jnp.asarray(by_window), returned)
    return pl.pallas_call(
        image_kernel,
        out_shape=shaped(2, 256, F, dtype=F32),
        in_specs=[VMEM] * (1 + N_COL),
        out_specs=HBM,
        scratch_shapes=[
            pltpu.VMEM((2, 256, F), F32),
            pltpu.VMEM((512, 512), BF),
            pltpu.SemaphoreType.DMA((PIECES,)),
        ],
        compiler_params=params(),
        cost_estimate=COST,
        name="image",
    )(jnp.asarray(by_column), *along_columns(back))


def solution(mesh):
    finer = Mesh(
        mesh.devices.reshape(4, 4, 2, mesh.shape["col"]), ("facet_0", "facet_1", "facet_2", "col")
    )
    return jax.shard_map(
        on_device,
        mesh=finer,
        in_specs=(P(None, FACET_COL, None), P(None, "col", None), P(None, "col", None), P("col")),
        out_specs=P(None, FACET_COL, None),
        check_vma=False,
    )
```

```python
import math

import jax
import jax.numpy as jnp
import ml_dtypes
import numpy as np
from jax import lax
from jax.experimental import pallas as pl
from jax.experimental.pallas import tpu as pltpu
from jax.sharding import Mesh
from jax.sharding import PartitionSpec as P

F = 1024
S = 512
IMAGE = 65536
VIS = 1024
W = 64
SUBCOL = 32
N_COL = 4
FACET = ("facet_0", "facet_1", "facet_2")
FACET_COL = ("facet_0", "facet_1", "facet_2", "col")
BF = jnp.bfloat16
F32 = jnp.float32
PIECES = 4
CHUNK = 256
COST = pl.CostEstimate(flops=2 * 10**10, bytes_accessed=2**24, transcendentals=0)


def unit(ticks, modulus):
    angle = (ticks % modulus).astype(np.float64) * (-2.0 * math.pi / modulus)
    return np.cos(angle), np.sin(angle)


def taper():
    return 0.6 + 0.4 * np.sin(math.pi * (np.arange(F) + 0.5) / F) ** 2


def bf(values):
    return np.asarray(values, np.float32).astype(ml_dtypes.bfloat16)


def hi_lo(values):
    high = bf(values)
    return high, bf(values - high.astype(np.float64))


def column_rows():
    c, l, q = np.arange(N_COL), np.arange(W), np.arange(F)
    vc = c * (IMAGE // 4) + (29 * c + 3) % 64
    ticks = q[None, None, :] * (vc[:, None, None] + 64 * l[None, :, None])
    real, imag = unit(ticks, IMAGE)
    weights = taper() / math.sqrt(F)
    return bf(np.stack([real * weights, imag * weights], axis=1).reshape(N_COL * 2 * W, F))


def window_rows():
    j, k, p = np.arange(SUBCOL), np.arange(W), np.arange(F)
    freqs = 1024 * (k[None, :] + j[:, None]) + ((37 * j + 5) % 1024)[:, None]
    real, imag = unit(p[None, None, :] * freqs[:, :, None], IMAGE)
    weights = taper() / math.sqrt(F)
    return bf(np.stack([real * weights, imag * weights], axis=1).reshape(SUBCOL * 128, F))


def left_rows():
    parts = unit(np.arange(256)[:, None] * np.arange(S)[None, :], S)
    return bf(np.stack([part.reshape(4, W, S) for part in parts], axis=1).reshape(S, S))


def right_rows():
    base = hi_lo(np.concatenate(unit(np.arange(W)[:, None] * np.arange(S)[None, :], S)))
    eighth = hi_lo(np.concatenate(unit(W * np.arange(8)[:, None] * np.arange(S)[None, :], S)))
    return np.concatenate([base[0], base[1], eighth[0], eighth[1]])


def facet_tables():
    return np.stack(unit(np.arange(W), W)).astype(np.float32)


def dot(a, b):
    return jnp.dot(a, b, preferred_element_type=F32)


def half_sign(shape):
    lane = lax.broadcasted_iota(jnp.int32, shape, len(shape) - 1)
    return jnp.where(lane % 128 < W, -1.0, 1.0).astype(F32)


def swap(values):
    return pltpu.roll(values, W, 1)


def scalar_phase(units, facet_row, facet_col, subgrid, column):
    shift = (37 * subgrid + 5) & 1023
    anchor = (29 * column + 3) & 63
    tick = (facet_row * shift + facet_col * anchor) & 63
    return units[0, tick], units[1, tick]


def column_of(shift):
    return (lax.axis_index("col") + shift) & (N_COL - 1)


def lanes(block, width):
    return pl.ds(pl.multiple_of(block * width, width), width)


def rows(block, height):
    return pl.ds(pl.multiple_of(block * height, height), height)


def strip_kernel(pixels, table, *refs):
    outs, held = refs[:N_COL], refs[N_COL]
    for part in range(2):
        held[part] = lax.dot_general(
            table[...], pixels[part], (((1,), (1,)), ((), ())), preferred_element_type=F32
        )
    for shift, out in enumerate(outs):
        at = rows(column_of(shift), 128)
        real, imag = held[0, at], held[1, at]
        out[:W] = (real[:W] - imag[W:]).astype(BF)
        out[W:] = (real[W:] + imag[:W]).astype(BF)


def window_kernel(units, table, after, *refs):
    strips = refs[:N_COL]
    out, turned = refs[N_COL:]
    facet = lax.axis_index(FACET)
    column = lax.axis_index("col")
    for shift, strip in enumerate(strips):
        turned[:, lanes(column_of(-shift), 256)] = strip[...]
    sign = half_sign((W, 128))
    group = 2
    for step in range(SUBCOL // group):
        both = dot(turned[...], table[:, step * group * 128 : (step + 1) * group * 128])
        for g in range(group):
            at = slice(g * 128, (g + 1) * 128)
            block = both[:W, at] + sign * swap(both[W:, at])
            real, imag = scalar_phase(units, facet // 8, facet % 8, step * group + g, column)
            out[step * group + g] = (block * real + sign * swap(block) * imag).astype(BF)


def wave_kernel(cells, left_tab, right_tab, left, base, eighth):
    subgrid = lax.axis_index(FACET)
    for begin in range(0, VIS, CHUNK):
        at = slice(begin, begin + CHUNK)
        first = cells[0, pl.ds(subgrid, 1), at]
        second = cells[1, pl.ds(subgrid, 1), at]
        cell = lax.broadcasted_iota(jnp.int32, (S, CHUNK), 0)
        picked = dot(left_tab[...], jnp.where(cell == first, 1.0, 0.0).astype(BF))
        left[:S, at] = picked.astype(BF)
        half, slot = begin // S, begin % S
        left[S + slot : S + slot + CHUNK, half * S : (half + 1) * S] = picked.T.astype(BF)
        right = dot(right_tab[...], jnp.where(cell == second, 1.0, 0.0).astype(BF))
        base[:, at] = right[0:128] + right[128:256]
        eighth[:, at] = right[256:272] + right[272:288]


def subgrid_kernel(
    units, counts, windows, observed, left, base, eighth, out, turned, weighted
):
    subgrid = lax.axis_index(FACET)
    column = lax.axis_index("col")
    count = counts[subgrid]
    sign = half_sign((W, 128))
    for x in range(4):
        for y in range(8):
            block = windows[x * 8 + y].astype(F32)
            at = slice(x * 128, (x + 1) * 128)
            turned[y * 128 : y * 128 + W, at] = (-sign * block).astype(BF)
            turned[y * 128 + W : (y + 1) * 128, at] = swap(block).astype(BF)
    for begin in range(0, VIS, CHUNK):
        at = slice(begin, begin + CHUNK)
        left_part = left[:S, at]
        base_real, base_imag = base[:W, at], base[W:, at]
        pred_real = jnp.zeros((1, CHUNK), F32)
        pred_imag = jnp.zeros((1, CHUNK), F32)
        for y in range(8):
            inner = dot(turned[y * 128 : (y + 1) * 128], left_part)
            inner_real, inner_imag = inner[:W], inner[W:]
            part_real = jnp.sum(inner_real * base_real - inner_imag * base_imag, axis=0, keepdims=True)
            part_imag = jnp.sum(inner_real * base_imag + inner_imag * base_real, axis=0, keepdims=True)
            er, ei = eighth[y : y + 1, at], eighth[8 + y : 9 + y, at]
            pred_real += part_real * er - part_imag * ei
            pred_imag += part_real * ei + part_imag * er
        slot = begin + lax.broadcasted_iota(jnp.int32, (1, CHUNK), 1)
        live = slot < count
        resid_real = jnp.where(live, observed[0, pl.ds(subgrid, 1), at] - pred_real / S, 0.0)
        resid_imag = jnp.where(live, observed[1, pl.ds(subgrid, 1), at] - pred_imag / S, 0.0)
        for y in range(8):
            er, ei = eighth[y : y + 1, at], eighth[8 + y : 9 + y, at]
            turned_real = resid_real * er + resid_imag * ei
            turned_imag = resid_imag * er - resid_real * ei
            weighted[y * 128 : y * 128 + W, at] = (
                turned_real * base_real + turned_imag * base_imag
            ).astype(BF)
            weighted[y * 128 + W : (y + 1) * 128, at] = (
                turned_imag * base_real - turned_real * base_imag
            ).astype(BF)
    scale = 1.0 / math.sqrt(VIS)
    for pair in range(4):
        part = weighted[pair * 256 : (pair + 1) * 256]
        both = dot(part[:, :S], left[S:, :S]) + dot(part[:, S:], left[S:, S:])
        for half in range(2):
            y = pair * 2 + half
            for x in range(4):
                at = slice(x * 128, (x + 1) * 128)
                upper = both[half * 128 : half * 128 + W, at]
                lower = both[half * 128 + W : (half + 1) * 128, at]
                block = swap(lower) - sign * upper
                real, imag = scalar_phase(units, x, y, subgrid, column)
                out[x * 8 + y] = (
                    block * (real * scale) - sign * swap(block) * (imag * scale)
                ).astype(BF)


def back_kernel(returned, *refs):
    tables, outs, turned = refs[: -N_COL - 1], refs[-N_COL - 1 : -1], refs[-1]
    sign = half_sign((W, 128))
    for j in range(SUBCOL):
        at = slice(j * 128, (j + 1) * 128)
        block = returned[j]
        turned[:W, at] = block
        turned[W:, at] = (-sign * swap(block.astype(F32))).astype(BF)
    depth = SUBCOL * 128 // len(tables)
    for shift, out in enumerate(outs):
        at = lanes(column_of(shift), 256)
        out[...] = sum(
            dot(turned[:, g * depth : (g + 1) * depth], table[:, at])
            for g, table in enumerate(tables)
        ).astype(BF)


def image_kernel(table, *refs):
    strips = refs[:N_COL]
    out, held, wide, left = refs[N_COL:]
    for shift, strip in enumerate(strips):
        at = lanes(column_of(-shift), 128)
        block = strip[...].astype(F32)
        other = jnp.concatenate([block[W:], -block[:W]], axis=0)
        wide[:256, at] = block.T.astype(BF)
        wide[256:, at] = other.T.astype(BF)
    copies = []
    for i in range(PIECES):
        at = slice(i * 256, (i + 1) * 256)
        held[:, :, at] = dot(wide[...], table[:, at]).reshape(2, 256, 256)
        copy = pltpu.make_async_copy(held.at[:, :, at], out.at[:, :, at], left.at[i])
        copy.start()
        copies.append(copy)
    for copy in copies:
        copy.wait()


VMEM = pl.BlockSpec(memory_space=pltpu.VMEM)
SMEM = pl.BlockSpec(memory_space=pltpu.SMEM)
HBM = pl.BlockSpec(memory_space=pltpu.HBM)


def params(mebibytes=24):
    return pltpu.CompilerParams(vmem_limit_bytes=mebibytes * 1024 * 1024)


def along_columns(parts):
    arrived = list(parts)
    for shift in (2, 1, 3):
        route = [(i, (i + shift) % N_COL) for i in range(N_COL)]
        arrived[shift] = lax.ppermute(parts[shift], "col", route)
    return arrived


def shaped(*dims, dtype=BF):
    return jax.ShapeDtypeStruct(dims, dtype)


def on_device(facets, observed, uv_cells, counts):
    units = jnp.asarray(facet_tables())
    by_column = jnp.asarray(column_rows())
    by_window = window_rows()
    back_tabs = [jnp.asarray(part) for part in np.split(by_window, 2)]
    strips = pl.pallas_call(
        strip_kernel,
        out_shape=[shaped(128, 256)] * N_COL,
        in_specs=[VMEM, VMEM],
        out_specs=[VMEM] * N_COL,
        scratch_shapes=[pltpu.VMEM((2, 512, 256), F32)],
        compiler_params=params(),
        cost_estimate=COST,
        name="strip",
    )(facets, by_column)
    waves = pl.pallas_call(
        wave_kernel,
        out_shape=[
            shaped(2 * S, VIS),
            shaped(128, VIS, dtype=F32),
            shaped(16, VIS, dtype=F32),
        ],
        in_specs=[VMEM] * 3,
        out_specs=[VMEM] * 3,
        compiler_params=params(),
        cost_estimate=COST,
        name="wave",
    )(uv_cells, jnp.asarray(left_rows()), jnp.asarray(right_rows()))
    windows = pl.pallas_call(
        window_kernel,
        out_shape=shaped(SUBCOL, W, 128),
        in_specs=[SMEM, VMEM, pl.BlockSpec(memory_space=pl.ANY)] + [VMEM] * N_COL,
        out_specs=VMEM,
        scratch_shapes=[pltpu.VMEM((128, F), BF)],
        compiler_params=params(),
        cost_estimate=COST,
        name="window",
    )(units, jnp.asarray(np.ascontiguousarray(by_window.T)), waves[-1], *along_columns(strips))
    windows = lax.all_to_all(windows, FACET, split_axis=0, concat_axis=0, tiled=True)
    returned = pl.pallas_call(
        subgrid_kernel,
        out_shape=shaped(SUBCOL, W, 128),
        in_specs=[SMEM, SMEM] + [VMEM] * 5,
        out_specs=VMEM,
        scratch_shapes=[pltpu.VMEM((1024, S), BF), pltpu.VMEM((1024, VIS), BF)],
        compiler_params=params(),
        cost_estimate=COST,
        name="subgrid",
    )(units, counts, windows, observed, *waves)
    returned = lax.all_to_all(returned, FACET, split_axis=0, concat_axis=0, tiled=True)
    back = pl.pallas_call(
        back_kernel,
        out_shape=[shaped(128, 256)] * N_COL,
        in_specs=[VMEM] * (1 + len(back_tabs)),
        out_specs=[VMEM] * N_COL,
        scratch_shapes=[pltpu.VMEM((128, SUBCOL * 128), BF)],
        compiler_params=params(),
        cost_estimate=COST,
        name="back",
    )(returned, *back_tabs)
    return pl.pallas_call(
        image_kernel,
        out_shape=shaped(2, 256, F, dtype=F32),
        in_specs=[VMEM] * (1 + N_COL),
        out_specs=HBM,
        scratch_shapes=[
            pltpu.VMEM((2, 256, F), F32),
            pltpu.VMEM((512, 512), BF),
            pltpu.SemaphoreType.DMA((PIECES,)),
        ],
        compiler_params=params(),
        cost_estimate=COST,
        name="image",
    )(by_column, *along_columns(back))


def solution(mesh):
    finer = Mesh(
        mesh.devices.reshape(4, 4, 2, mesh.shape["col"]), ("facet_0", "facet_1", "facet_2", "col")
    )
    return jax.shard_map(
        on_device,
        mesh=finer,
        in_specs=(P(None, FACET_COL, None), P(None, "col", None), P(None, "col", None), P("col")),
        out_specs=P(None, FACET_COL, None),
        check_vma=False,
    )
```

```python
import math

import jax
import jax.numpy as jnp
import ml_dtypes
import numpy as np
from jax import lax
from jax.experimental import pallas as pl
from jax.experimental.pallas import tpu as pltpu
from jax.sharding import Mesh
from jax.sharding import PartitionSpec as P

F = 1024
S = 512
IMAGE = 65536
VIS = 1024
W = 64
SUBCOL = 32
N_COL = 4
FACET = ("facet_0", "facet_1", "facet_2")
FACET_COL = ("facet_0", "facet_1", "facet_2", "col")
BF = jnp.bfloat16
F32 = jnp.float32
PIECES = 4
CHUNK = 256
GROUP = 4
COST = pl.CostEstimate(flops=2 * 10**10, bytes_accessed=2**24, transcendentals=0)


def unit(ticks, modulus):
    angle = (ticks % modulus).astype(np.float64) * (-2.0 * math.pi / modulus)
    return np.cos(angle), np.sin(angle)


def taper():
    return 0.6 + 0.4 * np.sin(math.pi * (np.arange(F) + 0.5) / F) ** 2


def bf(values):
    return np.asarray(values, np.float32).astype(ml_dtypes.bfloat16)


def hi_lo(values):
    high = bf(values)
    return high, bf(values - high.astype(np.float64))


def column_rows():
    c, l, q = np.arange(N_COL), np.arange(W), np.arange(F)
    vc = c * (IMAGE // 4) + (29 * c + 3) % 64
    ticks = q[None, None, :] * (vc[:, None, None] + 64 * l[None, :, None])
    real, imag = unit(ticks, IMAGE)
    weights = taper() / math.sqrt(F)
    return bf(np.stack([real * weights, imag * weights], axis=1).reshape(N_COL * 2 * W, F))


def window_rows():
    j, k, p = np.arange(SUBCOL), np.arange(W), np.arange(F)
    freqs = 1024 * (k[None, :] + j[:, None]) + ((37 * j + 5) % 1024)[:, None]
    real, imag = unit(p[None, None, :] * freqs[:, :, None], IMAGE)
    weights = taper() / math.sqrt(F)
    return bf(np.stack([real * weights, imag * weights], axis=1).reshape(SUBCOL * 128, F))


def left_rows():
    real, imag = unit(np.arange(256)[:, None] * np.arange(S)[None, :], S)
    return bf(np.stack([real.reshape(4, W, S), -imag.reshape(4, W, S)], axis=1).reshape(S, S))


def right_rows():
    base = hi_lo(np.concatenate(unit(np.arange(W)[:, None] * np.arange(S)[None, :], S)))
    eighth = hi_lo(np.concatenate(unit(W * np.arange(8)[:, None] * np.arange(S)[None, :], S)))
    return np.concatenate([base[0], base[1], eighth[0], eighth[1]])


def facet_tables():
    return np.stack(unit(np.arange(W), W)).astype(np.float32)


def dot(a, b):
    return jnp.dot(a, b, preferred_element_type=F32)


def half_sign(shape):
    lane = lax.broadcasted_iota(jnp.int32, shape, len(shape) - 1)
    return jnp.where(lane % 128 < W, -1.0, 1.0).astype(F32)


def swap(values):
    return pltpu.roll(values, W, 1)


def scalar_phase(units, facet_row, facet_col, subgrid, column):
    shift = (37 * subgrid + 5) & 1023
    anchor = (29 * column + 3) & 63
    tick = (facet_row * shift + facet_col * anchor) & 63
    return units[0, tick], units[1, tick]


def column_of(shift):
    return (lax.axis_index("col") + shift) & (N_COL - 1)


def lanes(block, width):
    return pl.ds(pl.multiple_of(block * width, width), width)


def rows(block, height):
    return pl.ds(pl.multiple_of(block * height, height), height)


def strip_kernel(pixels, table, *refs):
    outs = refs[:N_COL]
    pixels_in, table_in, held, arrived = refs[N_COL:]
    copies = []
    for i in range(PIECES):
        at = slice(i * F // PIECES, (i + 1) * F // PIECES)
        copies.append(pltpu.make_async_copy(table.at[:, at], table_in.at[:, at], arrived.at[i]))
        copies.append(
            pltpu.make_async_copy(
                pixels.at[:, :, at], pixels_in.at[:, :, at], arrived.at[PIECES + i]
            )
        )
    for copy in copies:
        copy.start()
    for i in range(PIECES):
        at = slice(i * F // PIECES, (i + 1) * F // PIECES)
        copies[2 * i].wait()
        copies[2 * i + 1].wait()
        for part in range(2):
            product = lax.dot_general(
                table_in[:, at],
                pixels_in[part, :, at],
                (((1,), (1,)), ((), ())),
                preferred_element_type=F32,
            )
            held[part] = product if i == 0 else held[part] + product
    for shift, out in enumerate(outs):
        at = rows(column_of(shift), 128)
        real, imag = held[0, at], held[1, at]
        out[:W] = (real[:W] - imag[W:]).astype(BF)
        out[W:] = (real[W:] + imag[:W]).astype(BF)


def window_kernel(units, table, after, *refs):
    strips = refs[:N_COL]
    out, turned = refs[N_COL:]
    facet = lax.axis_index(FACET)
    column = lax.axis_index("col")
    for shift, strip in enumerate(strips):
        turned[:, lanes(column_of(-shift), 256)] = strip[...]
    sign = half_sign((W, 128))
    group = 2
    for step in range(SUBCOL // group):
        both = dot(turned[...], table[:, step * group * 128 : (step + 1) * group * 128])
        for g in range(group):
            at = slice(g * 128, (g + 1) * 128)
            block = both[:W, at] + sign * swap(both[W:, at])
            real, imag = scalar_phase(units, facet // 8, facet % 8, step * group + g, column)
            out[step * group + g] = (block * real + sign * swap(block) * imag).astype(BF)


def wave_kernel(cells, left_tab, right_tab, left, left_by_slot, base, eighth):
    subgrid = lax.axis_index(FACET)
    for begin in range(0, VIS, CHUNK):
        at = slice(begin, begin + CHUNK)
        first = cells[0, pl.ds(subgrid, 1), at]
        second = cells[1, pl.ds(subgrid, 1), at]
        cell = lax.broadcasted_iota(jnp.int32, (S, CHUNK), 0)
        picked = dot(left_tab[...], jnp.where(cell == first, 1.0, 0.0).astype(BF))
        other = jnp.concatenate(
            [
                part
                for x in range(4)
                for part in (-picked[x * 128 + W : (x + 1) * 128], picked[x * 128 : x * 128 + W])
            ],
            axis=0,
        )
        left[:S, at] = picked.astype(BF)
        left[S:, at] = other.astype(BF)
        left_by_slot[at] = picked.T.astype(BF)
        left_by_slot[VIS + begin : VIS + begin + CHUNK] = other.T.astype(BF)
        right = dot(right_tab[...], jnp.where(cell == second, 1.0, 0.0).astype(BF))
        base[:, at] = right[0:128] + right[128:256]
        eighth[:, at] = right[256:272] + right[272:288]


def subgrid_kernel(
    units, counts, windows, observed, left, left_by_slot, base, eighth, out, held, weighted
):
    subgrid = lax.axis_index(FACET)
    column = lax.axis_index("col")
    count = counts[subgrid]
    for x in range(4):
        for y in range(8):
            held[y * W : (y + 1) * W, x * 128 : (x + 1) * 128] = windows[x * 8 + y]
    for begin in range(0, VIS, CHUNK):
        at = slice(begin, begin + CHUNK)
        base_real, base_imag = base[:W, at], base[W:, at]
        pred_real = jnp.zeros((1, CHUNK), F32)
        pred_imag = jnp.zeros((1, CHUNK), F32)
        for y0 in range(0, 8, GROUP):
            real = dot(held[y0 * W : (y0 + GROUP) * W], left[:S, at])
            imag = dot(held[y0 * W : (y0 + GROUP) * W], left[S:, at])
            for y in range(y0, y0 + GROUP):
                inner_real = real[(y - y0) * W : (y - y0 + 1) * W]
                inner_imag = imag[(y - y0) * W : (y - y0 + 1) * W]
                part_real = jnp.sum(
                    inner_real * base_real - inner_imag * base_imag, axis=0, keepdims=True
                )
                part_imag = jnp.sum(
                    inner_real * base_imag + inner_imag * base_real, axis=0, keepdims=True
                )
                er, ei = eighth[y : y + 1, at], eighth[8 + y : 9 + y, at]
                pred_real += part_real * er - part_imag * ei
                pred_imag += part_real * ei + part_imag * er
        slot = begin + lax.broadcasted_iota(jnp.int32, (1, CHUNK), 1)
        live = slot < count
        resid_real = jnp.where(live, observed[0, pl.ds(subgrid, 1), at] - pred_real / S, 0.0)
        resid_imag = jnp.where(live, observed[1, pl.ds(subgrid, 1), at] - pred_imag / S, 0.0)
        for y in range(8):
            er, ei = eighth[y : y + 1, at], eighth[8 + y : 9 + y, at]
            turned_real = resid_real * er + resid_imag * ei
            turned_imag = resid_imag * er - resid_real * ei
            here = slice(y * W, (y + 1) * W)
            weighted[here, at] = (turned_real * base_real + turned_imag * base_imag).astype(BF)
            weighted[here, VIS + begin : VIS + begin + CHUNK] = (
                turned_imag * base_real - turned_real * base_imag
            ).astype(BF)
    sign = half_sign((W, 128))
    scale = 1.0 / math.sqrt(VIS)
    for y0 in range(0, 8, GROUP):
        both = dot(weighted[y0 * W : (y0 + GROUP) * W], left_by_slot[...])
        for y in range(y0, y0 + GROUP):
            for x in range(4):
                block = both[(y - y0) * W : (y - y0 + 1) * W, x * 128 : (x + 1) * 128]
                real, imag = scalar_phase(units, x, y, subgrid, column)
                out[x * 8 + y] = (
                    block * (real * scale) - sign * swap(block) * (imag * scale)
                ).astype(BF)


def back_kernel(returned, *refs):
    tables, outs, turned = refs[: -N_COL - 1], refs[-N_COL - 1 : -1], refs[-1]
    sign = half_sign((W, 128))
    for j in range(SUBCOL):
        at = slice(j * 128, (j + 1) * 128)
        block = returned[j]
        turned[:W, at] = block
        turned[W:, at] = (-sign * swap(block.astype(F32))).astype(BF)
    depth = SUBCOL * 128 // len(tables)
    for shift, out in enumerate(outs):
        at = lanes(column_of(shift), 256)
        out[...] = sum(
            dot(turned[:, g * depth : (g + 1) * depth], table[:, at])
            for g, table in enumerate(tables)
        ).astype(BF)


def image_kernel(table, *refs):
    strips = refs[:N_COL]
    out, held, wide, left = refs[N_COL:]
    copies = []
    for part in range(2):
        for shift, strip in enumerate(strips):
            block = strip[...].astype(F32)
            if part == 1:
                block = jnp.concatenate([block[W:], -block[:W]], axis=0)
            wide[part * 256 : (part + 1) * 256, lanes(column_of(-shift), 128)] = block.T.astype(BF)
        for i in range(2):
            at = slice(i * 128, (i + 1) * 128)
            held[part, at] = dot(wide[part * 256 + i * 128 : part * 256 + (i + 1) * 128], table[...])
            copy = pltpu.make_async_copy(
                held.at[part, at], out.at[part, at], left.at[part * 2 + i]
            )
            copy.start(priority=i)
            copies.append(copy)
    for copy in copies:
        copy.wait()


VMEM = pl.BlockSpec(memory_space=pltpu.VMEM)
SMEM = pl.BlockSpec(memory_space=pltpu.SMEM)
HBM = pl.BlockSpec(memory_space=pltpu.HBM)


def params(mebibytes=24):
    return pltpu.CompilerParams(vmem_limit_bytes=mebibytes * 1024 * 1024)


def along_columns(parts):
    arrived = list(parts)
    for shift in (2, 1, 3):
        route = [(i, (i + shift) % N_COL) for i in range(N_COL)]
        arrived[shift] = lax.ppermute(parts[shift], "col", route)
    return arrived


def shaped(*dims, dtype=BF):
    return jax.ShapeDtypeStruct(dims, dtype)


def on_device(facets, observed, uv_cells, counts):
    units = jnp.asarray(facet_tables())
    by_column = jnp.asarray(column_rows())
    by_window = window_rows()
    back_tabs = [jnp.asarray(part) for part in np.split(by_window, 2)]
    strips = pl.pallas_call(
        strip_kernel,
        out_shape=[shaped(128, 256)] * N_COL,
        in_specs=[HBM, HBM],
        out_specs=[VMEM] * N_COL,
        scratch_shapes=[
            pltpu.VMEM((2, 256, F), BF),
            pltpu.VMEM((512, F), BF),
            pltpu.VMEM((2, 512, 256), F32),
            pltpu.SemaphoreType.DMA((2 * PIECES,)),
        ],
        compiler_params=params(),
        cost_estimate=COST,
        name="strip",
    )(
        pltpu.with_memory_space_constraint(facets, pltpu.HBM),
        pltpu.with_memory_space_constraint(by_column, pltpu.HBM),
    )
    waves = pl.pallas_call(
        wave_kernel,
        out_shape=[
            shaped(2 * S, VIS),
            shaped(2 * VIS, S),
            shaped(128, VIS, dtype=F32),
            shaped(16, VIS, dtype=F32),
        ],
        in_specs=[VMEM] * 3,
        out_specs=[VMEM] * 4,
        compiler_params=params(),
        cost_estimate=COST,
        name="wave",
    )(uv_cells, jnp.asarray(left_rows()), jnp.asarray(right_rows()))
    windows = pl.pallas_call(
        window_kernel,
        out_shape=shaped(SUBCOL, W, 128),
        in_specs=[SMEM, VMEM, pl.BlockSpec(memory_space=pl.ANY)] + [VMEM] * N_COL,
        out_specs=VMEM,
        scratch_shapes=[pltpu.VMEM((128, F), BF)],
        compiler_params=params(),
        cost_estimate=COST,
        name="window",
    )(units, jnp.asarray(np.ascontiguousarray(by_window.T)), waves[-1], *along_columns(strips))
    windows = lax.all_to_all(windows, FACET, split_axis=0, concat_axis=0, tiled=True)
    returned = pl.pallas_call(
        subgrid_kernel,
        out_shape=shaped(SUBCOL, W, 128),
        in_specs=[SMEM, SMEM] + [VMEM] * 6,
        out_specs=VMEM,
        scratch_shapes=[pltpu.VMEM((S, S), BF), pltpu.VMEM((S, 2 * VIS), BF)],
        compiler_params=params(),
        cost_estimate=COST,
        name="subgrid",
    )(units, counts, windows, observed, *waves)
    returned = lax.all_to_all(returned, FACET, split_axis=0, concat_axis=0, tiled=True)
    back = pl.pallas_call(
        back_kernel,
        out_shape=[shaped(128, 256)] * N_COL,
        in_specs=[VMEM] * (1 + len(back_tabs)),
        out_specs=[VMEM] * N_COL,
        scratch_shapes=[pltpu.VMEM((128, SUBCOL * 128), BF)],
        compiler_params=params(),
        cost_estimate=COST,
        name="back",
    )(returned, *back_tabs)
    return pl.pallas_call(
        image_kernel,
        out_shape=shaped(2, 256, F, dtype=F32),
        in_specs=[VMEM] * (1 + N_COL),
        out_specs=HBM,
        scratch_shapes=[
            pltpu.VMEM((2, 256, F), F32),
            pltpu.VMEM((512, 512), BF),
            pltpu.SemaphoreType.DMA((PIECES,)),
        ],
        compiler_params=params(),
        cost_estimate=COST,
        name="image",
    )(by_column, *along_columns(back))


def solution(mesh):
    finer = Mesh(
        mesh.devices.reshape(4, 4, 2, mesh.shape["col"]), ("facet_0", "facet_1", "facet_2", "col")
    )
    return jax.shard_map(
        on_device,
        mesh=finer,
        in_specs=(P(None, FACET_COL, None), P(None, "col", None), P(None, "col", None), P("col")),
        out_specs=P(None, FACET_COL, None),
        check_vma=False,
    )
```

```python
import math

import jax
import jax.numpy as jnp
import ml_dtypes
import numpy as np
from jax import lax
from jax.experimental import pallas as pl
from jax.experimental.pallas import tpu as pltpu
from jax.sharding import Mesh
from jax.sharding import PartitionSpec as P

F = 1024
S = 512
IMAGE = 65536
VIS = 1024
W = 64
SUBCOL = 32
N_COL = 4
FACET = ("facet_0", "facet_1", "facet_2")
FACET_COL = ("facet_0", "facet_1", "facet_2", "col")
BF = jnp.bfloat16
F32 = jnp.float32
PIECES = 4
CHUNK = 256
GROUP = 4
COST = pl.CostEstimate(flops=2 * 10**10, bytes_accessed=2**24, transcendentals=0)


def unit(ticks, modulus):
    angle = (ticks % modulus).astype(np.float64) * (-2.0 * math.pi / modulus)
    return np.cos(angle), np.sin(angle)


def taper():
    return 0.6 + 0.4 * np.sin(math.pi * (np.arange(F) + 0.5) / F) ** 2


def bf(values):
    return np.asarray(values, np.float32).astype(ml_dtypes.bfloat16)


def hi_lo(values):
    high = bf(values)
    return high, bf(values - high.astype(np.float64))


def column_rows():
    c, l, q = np.arange(N_COL), np.arange(W), np.arange(F)
    vc = c * (IMAGE // 4) + (29 * c + 3) % 64
    ticks = q[None, None, :] * (vc[:, None, None] + 64 * l[None, :, None])
    real, imag = unit(ticks, IMAGE)
    weights = taper() / math.sqrt(F)
    return bf(np.stack([real * weights, imag * weights], axis=1).reshape(N_COL * 2 * W, F))


def window_rows():
    j, k, p = np.arange(SUBCOL), np.arange(W), np.arange(F)
    freqs = 1024 * (k[None, :] + j[:, None]) + ((37 * j + 5) % 1024)[:, None]
    real, imag = unit(p[None, None, :] * freqs[:, :, None], IMAGE)
    weights = taper() / math.sqrt(F)
    return bf(np.stack([real * weights, imag * weights], axis=1).reshape(SUBCOL * 128, F))


def left_rows():
    real, imag = unit(np.arange(256)[:, None] * np.arange(S)[None, :], S)
    both = np.stack([real.reshape(4, W, S), -imag.reshape(4, W, S)], axis=1)
    return np.concatenate(hi_lo(both.reshape(S, S)))


def right_rows():
    base = hi_lo(np.concatenate(unit(np.arange(W)[:, None] * np.arange(S)[None, :], S)))
    eighth = hi_lo(np.concatenate(unit(W * np.arange(8)[:, None] * np.arange(S)[None, :], S)))
    return np.concatenate([base[0], base[1], eighth[0], eighth[1]])


def facet_tables():
    return np.stack(unit(np.arange(W), W)).astype(np.float32)


def dot(a, b):
    return jnp.dot(a, b, preferred_element_type=F32)


def half_sign(shape):
    lane = lax.broadcasted_iota(jnp.int32, shape, len(shape) - 1)
    return jnp.where(lane % 128 < W, -1.0, 1.0).astype(F32)


def swap(values):
    return pltpu.roll(values, W, 1)


def scalar_phase(units, tick):
    return units[0, tick & 63], units[1, tick & 63]


def column_of(shift):
    return (lax.axis_index("col") + shift) & (N_COL - 1)


def lanes(block, width):
    return pl.ds(pl.multiple_of(block * width, width), width)


def rows(block, height):
    return pl.ds(pl.multiple_of(block * height, height), height)


def strip_kernel(pixels, table, *refs):
    outs = refs[:N_COL]
    pixels_in, table_in, held, arrived = refs[N_COL:]
    copies = []
    for i in range(PIECES):
        at = slice(i * F // PIECES, (i + 1) * F // PIECES)
        copies.append(pltpu.make_async_copy(table.at[:, at], table_in.at[:, at], arrived.at[i]))
        copies.append(
            pltpu.make_async_copy(
                pixels.at[:, :, at], pixels_in.at[:, :, at], arrived.at[PIECES + i]
            )
        )
    for copy in copies:
        copy.start()
    for i in range(PIECES):
        at = slice(i * F // PIECES, (i + 1) * F // PIECES)
        copies[2 * i].wait()
        copies[2 * i + 1].wait()
        for part in range(2):
            product = lax.dot_general(
                table_in[:, at],
                pixels_in[part, :, at],
                (((1,), (1,)), ((), ())),
                preferred_element_type=F32,
            )
            held[part] = product if i == 0 else held[part] + product
    for shift, out in enumerate(outs):
        at = rows(column_of(shift), 128)
        real, imag = held[0, at], held[1, at]
        out[:W] = (real[:W] - imag[W:]).astype(BF)
        out[W:] = (real[W:] + imag[:W]).astype(BF)


def window_kernel(table, after, *refs):
    strips = refs[:N_COL]
    out, turned = refs[N_COL:]
    for shift, strip in enumerate(strips):
        turned[:, lanes(column_of(-shift), 256)] = strip[...]
    sign = half_sign((W, 128))
    group = 2
    for step in range(SUBCOL // group):
        both = dot(turned[...], table[:, step * group * 128 : (step + 1) * group * 128])
        for g in range(group):
            at = slice(g * 128, (g + 1) * 128)
            out[step * group + g] = (both[:W, at] + sign * swap(both[W:, at])).astype(BF)


def wave_kernel(units, cells, left_tab, right_tab, left, left_by_slot, base, eighth):
    subgrid = lax.axis_index(FACET)
    shift = (37 * subgrid + 5) & 1023
    anchor = (29 * lax.axis_index("col") + 3) & 63
    for begin in range(0, VIS, CHUNK):
        at = slice(begin, begin + CHUNK)
        first = cells[0, pl.ds(subgrid, 1), at]
        second = cells[1, pl.ds(subgrid, 1), at]
        cell = lax.broadcasted_iota(jnp.int32, (S, CHUNK), 0)
        picked = dot(left_tab[...], jnp.where(cell == first, 1.0, 0.0).astype(BF))
        picked = picked[:S] + picked[S:]
        first_rows, second_rows = [], []
        for x in range(4):
            real, imag = scalar_phase(units, x * shift)
            upper = picked[x * 128 : x * 128 + W]
            lower = picked[x * 128 + W : (x + 1) * 128]
            turned_real = upper * real + lower * imag
            turned_imag = upper * imag - lower * real
            first_rows += [turned_real, -turned_imag]
            second_rows += [turned_imag, turned_real]
        picked = jnp.concatenate(first_rows, axis=0)
        other = jnp.concatenate(second_rows, axis=0)
        left[:S, at] = picked.astype(BF)
        left[S:, at] = other.astype(BF)
        left_by_slot[at] = picked.T.astype(BF)
        left_by_slot[VIS + begin : VIS + begin + CHUNK] = other.T.astype(BF)
        right = dot(right_tab[...], jnp.where(cell == second, 1.0, 0.0).astype(BF))
        base[:, at] = right[0:128] + right[128:256]
        for y in range(8):
            real, imag = scalar_phase(units, y * anchor)
            upper = right[256 + y : 257 + y] + right[272 + y : 273 + y]
            lower = right[264 + y : 265 + y] + right[280 + y : 281 + y]
            eighth[y : y + 1, at] = upper * real - lower * imag
            eighth[8 + y : 9 + y, at] = upper * imag + lower * real


def subgrid_kernel(
    counts, windows, observed, left, left_by_slot, base, eighth, out, held, weighted
):
    subgrid = lax.axis_index(FACET)
    count = counts[subgrid]
    for x in range(4):
        for y in range(8):
            held[y * W : (y + 1) * W, x * 128 : (x + 1) * 128] = windows[x * 8 + y]
    for begin in range(0, VIS, CHUNK):
        at = slice(begin, begin + CHUNK)
        base_real, base_imag = base[:W, at], base[W:, at]
        pred_real = jnp.zeros((1, CHUNK), F32)
        pred_imag = jnp.zeros((1, CHUNK), F32)
        for y0 in range(0, 8, GROUP):
            real = dot(held[y0 * W : (y0 + GROUP) * W], left[:S, at])
            imag = dot(held[y0 * W : (y0 + GROUP) * W], left[S:, at])
            for y in range(y0, y0 + GROUP):
                inner_real = real[(y - y0) * W : (y - y0 + 1) * W]
                inner_imag = imag[(y - y0) * W : (y - y0 + 1) * W]
                part_real = jnp.sum(
                    inner_real * base_real - inner_imag * base_imag, axis=0, keepdims=True
                )
                part_imag = jnp.sum(
                    inner_real * base_imag + inner_imag * base_real, axis=0, keepdims=True
                )
                er, ei = eighth[y : y + 1, at], eighth[8 + y : 9 + y, at]
                pred_real += part_real * er - part_imag * ei
                pred_imag += part_real * ei + part_imag * er
        slot = begin + lax.broadcasted_iota(jnp.int32, (1, CHUNK), 1)
        live = slot < count
        resid_real = jnp.where(live, observed[0, pl.ds(subgrid, 1), at] - pred_real / S, 0.0)
        resid_imag = jnp.where(live, observed[1, pl.ds(subgrid, 1), at] - pred_imag / S, 0.0)
        for y in range(8):
            er, ei = eighth[y : y + 1, at], eighth[8 + y : 9 + y, at]
            turned_real = resid_real * er + resid_imag * ei
            turned_imag = resid_imag * er - resid_real * ei
            here = slice(y * W, (y + 1) * W)
            weighted[here, at] = (turned_real * base_real + turned_imag * base_imag).astype(BF)
            weighted[here, VIS + begin : VIS + begin + CHUNK] = (
                turned_imag * base_real - turned_real * base_imag
            ).astype(BF)
    scale = 1.0 / math.sqrt(VIS)
    for y0 in range(0, 8, GROUP):
        both = dot(weighted[y0 * W : (y0 + GROUP) * W], left_by_slot[...])
        for y in range(y0, y0 + GROUP):
            for x in range(4):
                block = both[(y - y0) * W : (y - y0 + 1) * W, x * 128 : (x + 1) * 128]
                out[x * 8 + y] = (block * scale).astype(BF)


def back_kernel(returned, *refs):
    tables, outs, turned = refs[: -N_COL - 1], refs[-N_COL - 1 : -1], refs[-1]
    sign = half_sign((W, 128))
    for j in range(SUBCOL):
        at = slice(j * 128, (j + 1) * 128)
        block = returned[j]
        turned[:W, at] = block
        turned[W:, at] = (-sign * swap(block.astype(F32))).astype(BF)
    depth = SUBCOL * 128 // len(tables)
    for shift, out in enumerate(outs):
        at = lanes(column_of(shift), 256)
        out[...] = sum(
            dot(turned[:, g * depth : (g + 1) * depth], table[:, at])
            for g, table in enumerate(tables)
        ).astype(BF)


def image_kernel(table, *refs):
    strips = refs[:N_COL]
    out, held, wide, left = refs[N_COL:]
    copies = []
    for part in range(2):
        for shift, strip in enumerate(strips):
            block = strip[...].astype(F32)
            if part == 1:
                block = jnp.concatenate([block[W:], -block[:W]], axis=0)
            wide[part * 256 : (part + 1) * 256, lanes(column_of(-shift), 128)] = block.T.astype(BF)
        for i in range(2):
            at = slice(i * 128, (i + 1) * 128)
            held[part, at] = dot(wide[part * 256 + i * 128 : part * 256 + (i + 1) * 128], table[...])
            copy = pltpu.make_async_copy(
                held.at[part, at], out.at[part, at], left.at[part * 2 + i]
            )
            copy.start(priority=i)
            copies.append(copy)
    for copy in copies:
        copy.wait()


VMEM = pl.BlockSpec(memory_space=pltpu.VMEM)
SMEM = pl.BlockSpec(memory_space=pltpu.SMEM)
HBM = pl.BlockSpec(memory_space=pltpu.HBM)


def params(mebibytes=24):
    return pltpu.CompilerParams(vmem_limit_bytes=mebibytes * 1024 * 1024)


def along_columns(parts):
    arrived = list(parts)
    for shift in (2, 1, 3):
        route = [(i, (i + shift) % N_COL) for i in range(N_COL)]
        arrived[shift] = lax.ppermute(parts[shift], "col", route)
    return arrived


def shaped(*dims, dtype=BF):
    return jax.ShapeDtypeStruct(dims, dtype)


def on_device(facets, observed, uv_cells, counts):
    units = jnp.asarray(facet_tables())
    by_column = jnp.asarray(column_rows())
    by_window = window_rows()
    back_tabs = [jnp.asarray(part) for part in np.split(by_window, 2)]
    strips = pl.pallas_call(
        strip_kernel,
        out_shape=[shaped(128, 256)] * N_COL,
        in_specs=[HBM, HBM],
        out_specs=[VMEM] * N_COL,
        scratch_shapes=[
            pltpu.VMEM((2, 256, F), BF),
            pltpu.VMEM((512, F), BF),
            pltpu.VMEM((2, 512, 256), F32),
            pltpu.SemaphoreType.DMA((2 * PIECES,)),
        ],
        compiler_params=params(),
        cost_estimate=COST,
        name="strip",
    )(
        pltpu.with_memory_space_constraint(facets, pltpu.HBM),
        pltpu.with_memory_space_constraint(by_column, pltpu.HBM),
    )
    waves = pl.pallas_call(
        wave_kernel,
        out_shape=[
            shaped(2 * S, VIS),
            shaped(2 * VIS, S),
            shaped(128, VIS, dtype=F32),
            shaped(16, VIS, dtype=F32),
        ],
        in_specs=[SMEM] + [VMEM] * 3,
        out_specs=[VMEM] * 4,
        compiler_params=params(),
        cost_estimate=COST,
        name="wave",
    )(units, uv_cells, jnp.asarray(left_rows()), jnp.asarray(right_rows()))
    windows = pl.pallas_call(
        window_kernel,
        out_shape=shaped(SUBCOL, W, 128),
        in_specs=[VMEM, pl.BlockSpec(memory_space=pl.ANY)] + [VMEM] * N_COL,
        out_specs=VMEM,
        scratch_shapes=[pltpu.VMEM((128, F), BF)],
        compiler_params=params(),
        cost_estimate=COST,
        name="window",
    )(jnp.asarray(np.ascontiguousarray(by_window.T)), waves[-1], *along_columns(strips))
    windows = lax.all_to_all(windows, FACET, split_axis=0, concat_axis=0, tiled=True)
    returned = pl.pallas_call(
        subgrid_kernel,
        out_shape=shaped(SUBCOL, W, 128),
        in_specs=[SMEM] + [VMEM] * 6,
        out_specs=VMEM,
        scratch_shapes=[pltpu.VMEM((S, S), BF), pltpu.VMEM((S, 2 * VIS), BF)],
        compiler_params=params(),
        cost_estimate=COST,
        name="subgrid",
    )(counts, windows, observed, *waves)
    returned = lax.all_to_all(returned, FACET, split_axis=0, concat_axis=0, tiled=True)
    back = pl.pallas_call(
        back_kernel,
        out_shape=[shaped(128, 256)] * N_COL,
        in_specs=[VMEM] * (1 + len(back_tabs)),
        out_specs=[VMEM] * N_COL,
        scratch_shapes=[pltpu.VMEM((128, SUBCOL * 128), BF)],
        compiler_params=params(),
        cost_estimate=COST,
        name="back",
    )(returned, *back_tabs)
    return pl.pallas_call(
        image_kernel,
        out_shape=shaped(2, 256, F, dtype=F32),
        in_specs=[VMEM] * (1 + N_COL),
        out_specs=HBM,
        scratch_shapes=[
            pltpu.VMEM((2, 256, F), F32),
            pltpu.VMEM((512, 512), BF),
            pltpu.SemaphoreType.DMA((PIECES,)),
        ],
        compiler_params=params(),
        cost_estimate=COST,
        name="image",
    )(by_column, *along_columns(back))


def solution(mesh):
    finer = Mesh(
        mesh.devices.reshape(4, 4, 2, mesh.shape["col"]), ("facet_0", "facet_1", "facet_2", "col")
    )
    return jax.shard_map(
        on_device,
        mesh=finer,
        in_specs=(P(None, FACET_COL, None), P(None, "col", None), P(None, "col", None), P("col")),
        out_specs=P(None, FACET_COL, None),
        check_vma=False,
    )
```

```python
import math

import jax
import jax.numpy as jnp
import ml_dtypes
import numpy as np
from jax import lax
from jax.experimental import pallas as pl
from jax.experimental.pallas import tpu as pltpu
from jax.sharding import Mesh
from jax.sharding import PartitionSpec as P

F = 1024
S = 512
IMAGE = 65536
VIS = 1024
W = 64
SUBCOL = 32
N_COL = 4
FACET = ("facet_0", "facet_1", "facet_2")
FACET_COL = ("facet_0", "facet_1", "facet_2", "col")
BF = jnp.bfloat16
F32 = jnp.float32
PIECES = 4
CHUNK = 256
GROUP = 4
ORDER = (0, 2, 1, 3)
COST = pl.CostEstimate(flops=2 * 10**10, bytes_accessed=2**24, transcendentals=0)


def unit(ticks, modulus):
    angle = (ticks % modulus).astype(np.float64) * (-2.0 * math.pi / modulus)
    return np.cos(angle), np.sin(angle)


def taper():
    return 0.6 + 0.4 * np.sin(math.pi * (np.arange(F) + 0.5) / F) ** 2


def bf(values):
    return np.asarray(values, np.float32).astype(ml_dtypes.bfloat16)


def hi_lo(values):
    high = bf(values)
    return high, bf(values - high.astype(np.float64))


def column_rows():
    c, l, q = np.arange(N_COL), np.arange(W), np.arange(F)
    vc = c * (IMAGE // 4) + (29 * c + 3) % 64
    ticks = q[None, None, :] * (vc[:, None, None] + 64 * l[None, :, None])
    real, imag = unit(ticks, IMAGE)
    weights = taper() / math.sqrt(F)
    return bf(np.stack([real * weights, imag * weights], axis=1).reshape(N_COL * 2 * W, F))


def window_rows():
    j, k, p = np.arange(SUBCOL), np.arange(W), np.arange(F)
    freqs = 1024 * (k[None, :] + j[:, None]) + ((37 * j + 5) % 1024)[:, None]
    real, imag = unit(p[None, None, :] * freqs[:, :, None], IMAGE)
    weights = taper() / math.sqrt(F)
    return bf(np.stack([real * weights, imag * weights], axis=1).reshape(SUBCOL * 128, F))


def left_rows():
    real, imag = unit(np.arange(256)[:, None] * np.arange(S)[None, :], S)
    both = np.stack([real.reshape(4, W, S), -imag.reshape(4, W, S)], axis=1)
    return np.concatenate(hi_lo(both.reshape(S, S)))


def right_rows():
    base = hi_lo(np.concatenate(unit(np.arange(W)[:, None] * np.arange(S)[None, :], S)))
    eighth = hi_lo(np.concatenate(unit(W * np.arange(8)[:, None] * np.arange(S)[None, :], S)))
    return np.concatenate([base[0], base[1], eighth[0], eighth[1]])


def facet_tables():
    return np.stack(unit(np.arange(W), W)).astype(np.float32)


def dot(a, b):
    return jnp.dot(a, b, preferred_element_type=F32)


def half_sign(shape):
    lane = lax.broadcasted_iota(jnp.int32, shape, len(shape) - 1)
    return jnp.where(lane % 128 < W, -1.0, 1.0).astype(F32)


def swap(values):
    return pltpu.roll(values, W, 1)


def scalar_phase(units, tick):
    return units[0, tick & 63], units[1, tick & 63]


def column_of(shift):
    return (lax.axis_index("col") + shift) & (N_COL - 1)


def lanes(block, width):
    return pl.ds(pl.multiple_of(block * width, width), width)


def rows(block, height):
    return pl.ds(pl.multiple_of(block * height, height), height)


def strip_kernel(pixels, table, *refs):
    outs = refs[:N_COL]
    pixels_in, table_in, held, arrived = refs[N_COL:]
    copies = []
    for i in range(PIECES):
        at = slice(i * F // PIECES, (i + 1) * F // PIECES)
        copies.append(pltpu.make_async_copy(table.at[:, at], table_in.at[:, at], arrived.at[i]))
        copies.append(
            pltpu.make_async_copy(
                pixels.at[:, :, at], pixels_in.at[:, :, at], arrived.at[PIECES + i]
            )
        )
    for copy in copies:
        copy.start()
    for i in range(PIECES):
        at = slice(i * F // PIECES, (i + 1) * F // PIECES)
        copies[2 * i].wait()
        copies[2 * i + 1].wait()
        for part in range(2):
            product = lax.dot_general(
                table_in[:, at],
                pixels_in[part, :, at],
                (((1,), (1,)), ((), ())),
                preferred_element_type=F32,
            )
            held[part] = product if i == 0 else held[part] + product
    for shift, out in enumerate(outs):
        at = rows(column_of(shift), 128)
        real, imag = held[0, at], held[1, at]
        out[:W] = (real[:W] - imag[W:]).astype(BF)
        out[W:] = (real[W:] + imag[:W]).astype(BF)


def window_kernel(table, after, *refs):
    strips = refs[:N_COL]
    out, turned = refs[N_COL:]
    for shift, strip in enumerate(strips):
        turned[:, lanes(column_of(-shift), 256)] = strip[...]
    sign = half_sign((W, 128))
    group = 2
    for step in range(SUBCOL // group):
        both = dot(turned[...], table[:, step * group * 128 : (step + 1) * group * 128])
        for g in range(group):
            at = slice(g * 128, (g + 1) * 128)
            out[step * group + g] = (both[:W, at] + sign * swap(both[W:, at])).astype(BF)


def wave_kernel(units, cells, left_tab, right_tab, left, left_by_slot, base, eighth):
    subgrid = lax.axis_index(FACET)
    shift = (37 * subgrid + 5) & 1023
    anchor = (29 * lax.axis_index("col") + 3) & 63
    for begin in range(0, VIS, CHUNK):
        at = slice(begin, begin + CHUNK)
        first = cells[0, pl.ds(subgrid, 1), at]
        second = cells[1, pl.ds(subgrid, 1), at]
        cell = lax.broadcasted_iota(jnp.int32, (S, CHUNK), 0)
        picked = dot(left_tab[...], jnp.where(cell == first, 1.0, 0.0).astype(BF))
        picked = picked[:S] + picked[S:]
        first_rows, second_rows = [], []
        for x in range(4):
            real, imag = scalar_phase(units, x * shift)
            upper = picked[x * 128 : x * 128 + W]
            lower = picked[x * 128 + W : (x + 1) * 128]
            turned_real = upper * real + lower * imag
            turned_imag = upper * imag - lower * real
            first_rows += [turned_real, -turned_imag]
            second_rows += [turned_imag, turned_real]
        picked = jnp.concatenate(first_rows, axis=0)
        other = jnp.concatenate(second_rows, axis=0)
        left[:S, at] = picked.astype(BF)
        left[S:, at] = other.astype(BF)
        left_by_slot[2 * begin : 2 * begin + CHUNK] = picked.T.astype(BF)
        left_by_slot[2 * begin + CHUNK : 2 * begin + 2 * CHUNK] = other.T.astype(BF)
        right = dot(right_tab[...], jnp.where(cell == second, 1.0, 0.0).astype(BF))
        base[:, at] = right[0:128] + right[128:256]
        for y in range(8):
            real, imag = scalar_phase(units, y * anchor)
            upper = right[256 + y : 257 + y] + right[272 + y : 273 + y]
            lower = right[264 + y : 265 + y] + right[280 + y : 281 + y]
            eighth[y : y + 1, at] = upper * real - lower * imag
            eighth[8 + y : 9 + y, at] = upper * imag + lower * real


def subgrid_kernel(
    counts, windows, observed, left, left_by_slot, base, eighth, out, held, weighted
):
    subgrid = lax.axis_index(FACET)
    count = counts[subgrid]
    for x in range(4):
        for y in range(8):
            held[y * W : (y + 1) * W, x * 128 : (x + 1) * 128] = windows[x * 8 + y]
    for begin in range(0, VIS, CHUNK):
        at = slice(begin, begin + CHUNK)
        base_real, base_imag = base[:W, at], base[W:, at]
        pred_real = jnp.zeros((1, CHUNK), F32)
        pred_imag = jnp.zeros((1, CHUNK), F32)
        for y0 in range(0, 8, GROUP):
            real = dot(held[y0 * W : (y0 + GROUP) * W], left[:S, at])
            imag = dot(held[y0 * W : (y0 + GROUP) * W], left[S:, at])
            for y in range(y0, y0 + GROUP):
                inner_real = real[(y - y0) * W : (y - y0 + 1) * W]
                inner_imag = imag[(y - y0) * W : (y - y0 + 1) * W]
                part_real = jnp.sum(
                    inner_real * base_real - inner_imag * base_imag, axis=0, keepdims=True
                )
                part_imag = jnp.sum(
                    inner_real * base_imag + inner_imag * base_real, axis=0, keepdims=True
                )
                er, ei = eighth[y : y + 1, at], eighth[8 + y : 9 + y, at]
                pred_real += part_real * er - part_imag * ei
                pred_imag += part_real * ei + part_imag * er
        slot = begin + lax.broadcasted_iota(jnp.int32, (1, CHUNK), 1)
        live = slot < count
        resid_real = jnp.where(live, observed[0, pl.ds(subgrid, 1), at] - pred_real / S, 0.0)
        resid_imag = jnp.where(live, observed[1, pl.ds(subgrid, 1), at] - pred_imag / S, 0.0)
        for y in range(8):
            er, ei = eighth[y : y + 1, at], eighth[8 + y : 9 + y, at]
            turned_real = resid_real * er + resid_imag * ei
            turned_imag = resid_imag * er - resid_real * ei
            here = slice(y * W, (y + 1) * W)
            weighted[here, 2 * begin : 2 * begin + CHUNK] = (
                turned_real * base_real + turned_imag * base_imag
            ).astype(BF)
            weighted[here, 2 * begin + CHUNK : 2 * begin + 2 * CHUNK] = (
                turned_imag * base_real - turned_real * base_imag
            ).astype(BF)
    scale = 1.0 / math.sqrt(VIS)
    both = dot(weighted[...], left_by_slot[...]) * scale
    for y in range(8):
        for x in range(4):
            out[x * 8 + y] = both[y * W : (y + 1) * W, x * 128 : (x + 1) * 128].astype(BF)


def back_kernel(returned, *refs):
    tables, outs, turned = refs[: -N_COL - 1], refs[-N_COL - 1 : -1], refs[-1]
    sign = half_sign((W, 128))
    for j in range(SUBCOL):
        at = slice(j * 128, (j + 1) * 128)
        block = returned[j]
        turned[:W, at] = block
        turned[W:, at] = (-sign * swap(block.astype(F32))).astype(BF)
    depth = SUBCOL * 128 // len(tables)
    for shift, out in enumerate(outs):
        at = lanes(column_of(shift), 256)
        out[...] = sum(
            dot(turned[:, g * depth : (g + 1) * depth], table[:, at])
            for g, table in enumerate(tables)
        ).astype(BF)


def image_kernel(table, *refs):
    strips = refs[:N_COL]
    out, held, wide, left = refs[N_COL:]
    copies = []
    for part in range(2):
        for shift, strip in zip(ORDER, strips):
            block = strip[...].astype(F32)
            if part == 1:
                block = jnp.concatenate([block[W:], -block[:W]], axis=0)
            wide[part * 256 : (part + 1) * 256, lanes(column_of(-shift), 128)] = block.T.astype(BF)
        for i in range(2):
            at = slice(i * 128, (i + 1) * 128)
            held[part, at] = dot(wide[part * 256 + i * 128 : part * 256 + (i + 1) * 128], table[...])
            copy = pltpu.make_async_copy(
                held.at[part, at], out.at[part, at], left.at[part * 2 + i]
            )
            copy.start(priority=i)
            copies.append(copy)
    for copy in copies:
        copy.wait()


VMEM = pl.BlockSpec(memory_space=pltpu.VMEM)
SMEM = pl.BlockSpec(memory_space=pltpu.SMEM)
HBM = pl.BlockSpec(memory_space=pltpu.HBM)


def params(mebibytes=24):
    return pltpu.CompilerParams(vmem_limit_bytes=mebibytes * 1024 * 1024)


def along_columns(parts):
    arrived = list(parts)
    for shift in (2, 1, 3):
        route = [(i, (i + shift) % N_COL) for i in range(N_COL)]
        arrived[shift] = lax.ppermute(parts[shift], "col", route)
    return arrived


def in_order(parts):
    return [parts[shift] for shift in ORDER]


def shaped(*dims, dtype=BF):
    return jax.ShapeDtypeStruct(dims, dtype)


def on_device(facets, observed, uv_cells, counts):
    units = jnp.asarray(facet_tables())
    by_column = jnp.asarray(column_rows())
    by_window = window_rows()
    back_tabs = [jnp.asarray(part) for part in np.split(by_window, 2)]
    strips = pl.pallas_call(
        strip_kernel,
        out_shape=[shaped(128, 256)] * N_COL,
        in_specs=[HBM, HBM],
        out_specs=[VMEM] * N_COL,
        scratch_shapes=[
            pltpu.VMEM((2, 256, F), BF),
            pltpu.VMEM((512, F), BF),
            pltpu.VMEM((2, 512, 256), F32),
            pltpu.SemaphoreType.DMA((2 * PIECES,)),
        ],
        compiler_params=params(),
        cost_estimate=COST,
        name="strip",
    )(
        pltpu.with_memory_space_constraint(facets, pltpu.HBM),
        pltpu.with_memory_space_constraint(by_column, pltpu.HBM),
    )
    waves = pl.pallas_call(
        wave_kernel,
        out_shape=[
            shaped(2 * S, VIS),
            shaped(2 * VIS, S),
            shaped(128, VIS, dtype=F32),
            shaped(16, VIS, dtype=F32),
        ],
        in_specs=[SMEM] + [VMEM] * 3,
        out_specs=[VMEM] * 4,
        compiler_params=params(),
        cost_estimate=COST,
        name="wave",
    )(units, uv_cells, jnp.asarray(left_rows()), jnp.asarray(right_rows()))
    windows = pl.pallas_call(
        window_kernel,
        out_shape=shaped(SUBCOL, W, 128),
        in_specs=[VMEM, pl.BlockSpec(memory_space=pl.ANY)] + [VMEM] * N_COL,
        out_specs=VMEM,
        scratch_shapes=[pltpu.VMEM((128, F), BF)],
        compiler_params=params(),
        cost_estimate=COST,
        name="window",
    )(jnp.asarray(np.ascontiguousarray(by_window.T)), waves[-1], *along_columns(strips))
    windows = lax.all_to_all(windows, FACET, split_axis=0, concat_axis=0, tiled=True)
    returned = pl.pallas_call(
        subgrid_kernel,
        out_shape=shaped(SUBCOL, W, 128),
        in_specs=[SMEM] + [VMEM] * 6,
        out_specs=VMEM,
        scratch_shapes=[pltpu.VMEM((S, S), BF), pltpu.VMEM((S, 2 * VIS), BF)],
        compiler_params=params(),
        cost_estimate=COST,
        name="subgrid",
    )(counts, windows, observed, *waves)
    returned = lax.all_to_all(returned, FACET, split_axis=0, concat_axis=0, tiled=True)
    back = pl.pallas_call(
        back_kernel,
        out_shape=[shaped(128, 256)] * N_COL,
        in_specs=[VMEM] * (1 + len(back_tabs)),
        out_specs=[VMEM] * N_COL,
        scratch_shapes=[pltpu.VMEM((128, SUBCOL * 128), BF)],
        compiler_params=params(),
        cost_estimate=COST,
        name="back",
    )(returned, *back_tabs)
    return pl.pallas_call(
        image_kernel,
        out_shape=shaped(2, 256, F, dtype=F32),
        in_specs=[VMEM] * (1 + N_COL),
        out_specs=HBM,
        scratch_shapes=[
            pltpu.VMEM((2, 256, F), F32),
            pltpu.VMEM((512, 512), BF),
            pltpu.SemaphoreType.DMA((PIECES,)),
        ],
        compiler_params=params(),
        cost_estimate=COST,
        name="image",
    )(by_column, *in_order(along_columns(back)))


def solution(mesh):
    finer = Mesh(
        mesh.devices.reshape(4, 4, 2, mesh.shape["col"]), ("facet_0", "facet_1", "facet_2", "col")
    )
    return jax.shard_map(
        on_device,
        mesh=finer,
        in_specs=(P(None, FACET_COL, None), P(None, "col", None), P(None, "col", None), P("col")),
        out_specs=P(None, FACET_COL, None),
        check_vma=False,
    )
```

```python
import math

import jax
import jax.numpy as jnp
import ml_dtypes
import numpy as np
from jax import lax
from jax.experimental import pallas as pl
from jax.experimental.pallas import tpu as pltpu
from jax.sharding import Mesh
from jax.sharding import PartitionSpec as P

F = 1024
S = 512
IMAGE = 65536
VIS = 1024
W = 64
SUBCOL = 32
N_COL = 4
FACET = ("facet_0", "facet_1", "facet_2")
FACET_COL = ("facet_0", "facet_1", "facet_2", "col")
BF = jnp.bfloat16
F32 = jnp.float32
PIECES = 4
CHUNK = 256
GROUP = 4
ORDER = (0, 2, 1, 3)
COST = pl.CostEstimate(flops=2 * 10**10, bytes_accessed=2**24, transcendentals=0)


def unit(ticks, modulus):
    angle = (ticks % modulus).astype(np.float64) * (-2.0 * math.pi / modulus)
    return np.cos(angle), np.sin(angle)


def taper():
    return 0.6 + 0.4 * np.sin(math.pi * (np.arange(F) + 0.5) / F) ** 2


def bf(values):
    return np.asarray(values, np.float32).astype(ml_dtypes.bfloat16)


def hi_lo(values):
    high = bf(values)
    return high, bf(values - high.astype(np.float64))


def column_rows():
    c, l, q = np.arange(N_COL), np.arange(W), np.arange(F)
    vc = c * (IMAGE // 4) + (29 * c + 3) % 64
    ticks = q[None, None, :] * (vc[:, None, None] + 64 * l[None, :, None])
    real, imag = unit(ticks, IMAGE)
    weights = taper() / math.sqrt(F)
    return bf(np.stack([real * weights, imag * weights], axis=1).reshape(N_COL * 2 * W, F))


def window_rows():
    j, k, p = np.arange(SUBCOL), np.arange(W), np.arange(F)
    freqs = 1024 * (k[None, :] + j[:, None]) + ((37 * j + 5) % 1024)[:, None]
    real, imag = unit(p[None, None, :] * freqs[:, :, None], IMAGE)
    weights = taper() / math.sqrt(F)
    return bf(np.stack([real * weights, imag * weights], axis=1).reshape(SUBCOL * 128, F))


def left_rows():
    real, imag = unit(np.arange(256)[:, None] * np.arange(S)[None, :], S)
    both = np.stack([real.reshape(4, W, S), -imag.reshape(4, W, S)], axis=1)
    return np.concatenate(hi_lo(both.reshape(S, S)))


def right_rows():
    base = hi_lo(np.concatenate(unit(np.arange(W)[:, None] * np.arange(S)[None, :], S)))
    eighth = hi_lo(np.concatenate(unit(W * np.arange(8)[:, None] * np.arange(S)[None, :], S)))
    return np.concatenate([base[0], base[1], eighth[0], eighth[1]])


def facet_tables():
    return np.stack(unit(np.arange(W), W)).astype(np.float32)


def dot(a, b):
    return jnp.dot(a, b, preferred_element_type=F32)


def half_sign(shape):
    lane = lax.broadcasted_iota(jnp.int32, shape, len(shape) - 1)
    return jnp.where(lane % 128 < W, -1.0, 1.0).astype(F32)


def swap(values):
    return pltpu.roll(values, W, 1)


def scalar_phase(units, tick):
    return units[0, tick & 63], units[1, tick & 63]


def column_of(shift):
    return (lax.axis_index("col") + shift) & (N_COL - 1)


def lanes(block, width):
    return pl.ds(pl.multiple_of(block * width, width), width)


def rows(block, height):
    return pl.ds(pl.multiple_of(block * height, height), height)


def strip_kernel(pixels, table, *refs):
    outs = refs[:N_COL]
    pixels_in, table_in, held, arrived = refs[N_COL:]
    copies = []
    for i in range(PIECES):
        at = slice(i * F // PIECES, (i + 1) * F // PIECES)
        copies.append(pltpu.make_async_copy(table.at[:, at], table_in.at[:, at], arrived.at[i]))
        copies.append(
            pltpu.make_async_copy(
                pixels.at[:, :, at], pixels_in.at[:, :, at], arrived.at[PIECES + i]
            )
        )
    for copy in copies:
        copy.start()
    for i in range(PIECES):
        at = slice(i * F // PIECES, (i + 1) * F // PIECES)
        copies[2 * i].wait()
        copies[2 * i + 1].wait()
        for part in range(2):
            product = lax.dot_general(
                table_in[:, at],
                pixels_in[part, :, at],
                (((1,), (1,)), ((), ())),
                preferred_element_type=F32,
            )
            held[part] = product if i == 0 else held[part] + product
    for shift, out in enumerate(outs):
        at = rows(column_of(shift), 128)
        real, imag = held[0, at], held[1, at]
        out[:W] = (real[:W] - imag[W:]).astype(BF)
        out[W:] = (real[W:] + imag[:W]).astype(BF)


def window_kernel(table, after, *refs):
    strips = refs[:N_COL]
    out, turned = refs[N_COL:]
    for shift, strip in enumerate(strips):
        turned[:, lanes(column_of(-shift), 256)] = strip[...]
    sign = half_sign((W, 128))
    group = 2
    for step in range(SUBCOL // group):
        both = dot(turned[...], table[:, step * group * 128 : (step + 1) * group * 128])
        for g in range(group):
            at = slice(g * 128, (g + 1) * 128)
            out[step * group + g] = (both[:W, at] + sign * swap(both[W:, at])).astype(BF)


def wave_kernel(units, cells, left_tab, right_tab, left, left_by_slot, base, eighth):
    subgrid = lax.axis_index(FACET)
    shift = (37 * subgrid + 5) & 1023
    anchor = (29 * lax.axis_index("col") + 3) & 63
    scale = 1.0 / math.sqrt(VIS)
    for begin in range(0, VIS, CHUNK):
        at = slice(begin, begin + CHUNK)
        first = cells[0, pl.ds(subgrid, 1), at]
        second = cells[1, pl.ds(subgrid, 1), at]
        cell = lax.broadcasted_iota(jnp.int32, (S, CHUNK), 0)
        picked = dot(left_tab[...], jnp.where(cell == first, 1.0, 0.0).astype(BF))
        picked = picked[:S] + picked[S:]
        first_rows, second_rows = [], []
        for x in range(4):
            real, imag = scalar_phase(units, x * shift)
            upper = picked[x * 128 : x * 128 + W]
            lower = picked[x * 128 + W : (x + 1) * 128]
            turned_real = upper * real + lower * imag
            turned_imag = upper * imag - lower * real
            first_rows += [turned_real, -turned_imag]
            second_rows += [turned_imag, turned_real]
        picked = jnp.concatenate(first_rows, axis=0)
        other = jnp.concatenate(second_rows, axis=0)
        left[:S, at] = picked.astype(BF)
        left[S:, at] = other.astype(BF)
        left_by_slot[2 * begin : 2 * begin + CHUNK] = (picked * scale).T.astype(BF)
        left_by_slot[2 * begin + CHUNK : 2 * begin + 2 * CHUNK] = (other * scale).T.astype(BF)
        right = dot(right_tab[...], jnp.where(cell == second, 1.0, 0.0).astype(BF))
        base[:, at] = right[0:128] + right[128:256]
        for y in range(8):
            real, imag = scalar_phase(units, y * anchor)
            upper = right[256 + y : 257 + y] + right[272 + y : 273 + y]
            lower = right[264 + y : 265 + y] + right[280 + y : 281 + y]
            eighth[y : y + 1, at] = upper * real - lower * imag
            eighth[8 + y : 9 + y, at] = upper * imag + lower * real


def subgrid_kernel(
    counts, windows, observed, left, left_by_slot, base, eighth, out, held, weighted
):
    subgrid = lax.axis_index(FACET)
    count = counts[subgrid]
    for x in range(4):
        for y in range(8):
            held[y * W : (y + 1) * W, x * 128 : (x + 1) * 128] = windows[x * 8 + y]
    for begin in range(0, VIS, CHUNK):
        at = slice(begin, begin + CHUNK)
        base_real, base_imag = base[:W, at], base[W:, at]
        pred_real = jnp.zeros((1, CHUNK), F32)
        pred_imag = jnp.zeros((1, CHUNK), F32)
        for y0 in range(0, 8, GROUP):
            real = dot(held[y0 * W : (y0 + GROUP) * W], left[:S, at])
            imag = dot(held[y0 * W : (y0 + GROUP) * W], left[S:, at])
            for y in range(y0, y0 + GROUP):
                inner_real = real[(y - y0) * W : (y - y0 + 1) * W]
                inner_imag = imag[(y - y0) * W : (y - y0 + 1) * W]
                part_real = jnp.sum(
                    inner_real * base_real - inner_imag * base_imag, axis=0, keepdims=True
                )
                part_imag = jnp.sum(
                    inner_real * base_imag + inner_imag * base_real, axis=0, keepdims=True
                )
                er, ei = eighth[y : y + 1, at], eighth[8 + y : 9 + y, at]
                pred_real += part_real * er - part_imag * ei
                pred_imag += part_real * ei + part_imag * er
        slot = begin + lax.broadcasted_iota(jnp.int32, (1, CHUNK), 1)
        live = slot < count
        resid_real = jnp.where(live, observed[0, pl.ds(subgrid, 1), at] - pred_real / S, 0.0)
        resid_imag = jnp.where(live, observed[1, pl.ds(subgrid, 1), at] - pred_imag / S, 0.0)
        for y in range(8):
            er, ei = eighth[y : y + 1, at], eighth[8 + y : 9 + y, at]
            turned_real = resid_real * er + resid_imag * ei
            turned_imag = resid_imag * er - resid_real * ei
            here = slice(y * W, (y + 1) * W)
            weighted[here, 2 * begin : 2 * begin + CHUNK] = (
                turned_real * base_real + turned_imag * base_imag
            ).astype(BF)
            weighted[here, 2 * begin + CHUNK : 2 * begin + 2 * CHUNK] = (
                turned_imag * base_real - turned_real * base_imag
            ).astype(BF)
    both = dot(weighted[...], left_by_slot[...])
    for y in range(8):
        for x in range(4):
            out[x * 8 + y] = both[y * W : (y + 1) * W, x * 128 : (x + 1) * 128].astype(BF)


def back_kernel(returned, *refs):
    tables, outs, turned = refs[: -N_COL - 1], refs[-N_COL - 1 : -1], refs[-1]
    sign = half_sign((W, 128))
    for j in range(SUBCOL):
        at = slice(j * 128, (j + 1) * 128)
        block = returned[j]
        turned[:W, at] = block
        turned[W:, at] = (-sign * swap(block.astype(F32))).astype(BF)
    depth = SUBCOL * 128 // len(tables)
    for shift, out in enumerate(outs):
        at = lanes(column_of(shift), 256)
        out[...] = sum(
            dot(turned[:, g * depth : (g + 1) * depth], table[:, at])
            for g, table in enumerate(tables)
        ).astype(BF)


def image_kernel(table, *refs):
    strips = refs[:N_COL]
    out, held, wide, left = refs[N_COL:]
    copies = []
    for part in range(2):
        for shift, strip in zip(ORDER, strips):
            block = strip[...].astype(F32)
            if part == 1:
                block = jnp.concatenate([block[W:], -block[:W]], axis=0)
            wide[part * 256 : (part + 1) * 256, lanes(column_of(-shift), 128)] = block.T.astype(BF)
        for i in range(2):
            at = slice(i * 128, (i + 1) * 128)
            held[part, at] = dot(wide[part * 256 + i * 128 : part * 256 + (i + 1) * 128], table[...])
            copy = pltpu.make_async_copy(
                held.at[part, at], out.at[part, at], left.at[part * 2 + i]
            )
            copy.start(priority=i)
            copies.append(copy)
    for copy in copies:
        copy.wait()


VMEM = pl.BlockSpec(memory_space=pltpu.VMEM)
SMEM = pl.BlockSpec(memory_space=pltpu.SMEM)
HBM = pl.BlockSpec(memory_space=pltpu.HBM)


def params(mebibytes=24):
    return pltpu.CompilerParams(vmem_limit_bytes=mebibytes * 1024 * 1024)


def along_columns(parts):
    arrived = list(parts)
    for shift in (2, 1, 3):
        route = [(i, (i + shift) % N_COL) for i in range(N_COL)]
        arrived[shift] = lax.ppermute(parts[shift], "col", route)
    return arrived


def in_order(parts):
    return [parts[shift] for shift in ORDER]


def shaped(*dims, dtype=BF):
    return jax.ShapeDtypeStruct(dims, dtype)


def on_device(facets, observed, uv_cells, counts):
    units = jnp.asarray(facet_tables())
    by_column = jnp.asarray(column_rows())
    by_window = window_rows()
    back_tabs = [jnp.asarray(part) for part in np.split(by_window, 2)]
    strips = pl.pallas_call(
        strip_kernel,
        out_shape=[shaped(128, 256)] * N_COL,
        in_specs=[HBM, HBM],
        out_specs=[VMEM] * N_COL,
        scratch_shapes=[
            pltpu.VMEM((2, 256, F), BF),
            pltpu.VMEM((512, F), BF),
            pltpu.VMEM((2, 512, 256), F32),
            pltpu.SemaphoreType.DMA((2 * PIECES,)),
        ],
        compiler_params=params(),
        cost_estimate=COST,
        name="strip",
    )(
        pltpu.with_memory_space_constraint(facets, pltpu.HBM),
        pltpu.with_memory_space_constraint(by_column, pltpu.HBM),
    )
    waves = pl.pallas_call(
        wave_kernel,
        out_shape=[
            shaped(2 * S, VIS),
            shaped(2 * VIS, S),
            shaped(128, VIS, dtype=F32),
            shaped(16, VIS, dtype=F32),
        ],
        in_specs=[SMEM] + [VMEM] * 3,
        out_specs=[VMEM] * 4,
        compiler_params=params(),
        cost_estimate=COST,
        name="wave",
    )(units, uv_cells, jnp.asarray(left_rows()), jnp.asarray(right_rows()))
    windows = pl.pallas_call(
        window_kernel,
        out_shape=shaped(SUBCOL, W, 128),
        in_specs=[VMEM, pl.BlockSpec(memory_space=pl.ANY)] + [VMEM] * N_COL,
        out_specs=VMEM,
        scratch_shapes=[pltpu.VMEM((128, F), BF)],
        compiler_params=params(),
        cost_estimate=COST,
        name="window",
    )(jnp.asarray(np.ascontiguousarray(by_window.T)), waves[-1], *along_columns(strips))
    windows = lax.all_to_all(windows, FACET, split_axis=0, concat_axis=0, tiled=True)
    returned = pl.pallas_call(
        subgrid_kernel,
        out_shape=shaped(SUBCOL, W, 128),
        in_specs=[SMEM] + [VMEM] * 6,
        out_specs=VMEM,
        scratch_shapes=[pltpu.VMEM((S, S), BF), pltpu.VMEM((S, 2 * VIS), BF)],
        compiler_params=params(),
        cost_estimate=COST,
        name="subgrid",
    )(counts, windows, observed, *waves)
    returned = lax.all_to_all(returned, FACET, split_axis=0, concat_axis=0, tiled=True)
    back = pl.pallas_call(
        back_kernel,
        out_shape=[shaped(128, 256)] * N_COL,
        in_specs=[VMEM] * (1 + len(back_tabs)),
        out_specs=[VMEM] * N_COL,
        scratch_shapes=[pltpu.VMEM((128, SUBCOL * 128), BF)],
        compiler_params=params(),
        cost_estimate=COST,
        name="back",
    )(returned, *back_tabs)
    return pl.pallas_call(
        image_kernel,
        out_shape=shaped(2, 256, F, dtype=F32),
        in_specs=[VMEM] * (1 + N_COL),
        out_specs=HBM,
        scratch_shapes=[
            pltpu.VMEM((2, 256, F), F32),
            pltpu.VMEM((512, 512), BF),
            pltpu.SemaphoreType.DMA((PIECES,)),
        ],
        compiler_params=params(),
        cost_estimate=COST,
        name="image",
    )(by_column, *in_order(along_columns(back)))


def solution(mesh):
    finer = Mesh(
        mesh.devices.reshape(4, 4, 2, mesh.shape["col"]), ("facet_0", "facet_1", "facet_2", "col")
    )
    return jax.shard_map(
        on_device,
        mesh=finer,
        in_specs=(P(None, FACET_COL, None), P(None, "col", None), P(None, "col", None), P("col")),
        out_specs=P(None, FACET_COL, None),
        check_vma=False,
    )
```
